32 devices in a mesh: dp: 16 (over z, y, x), mp: 2 (over core).
Axes of the slice: x: 2, y: 2, z: 4, core: 2. Of those that a mesh axis runs over, the one named last changes fastest.
Arguments:
- tokens: float32 [32768, 768], P('dp'), may hold values from -6 to 6
- latents: float32 [1024, 768], P('dp'), may hold values from -6 to 6
- condition: float32 [128, 768], P('dp'), may hold values from -6 to 6
- modulator: float32 [768, 4608], P('dp'), may hold values from -0.21875 to 0.21875
- offsets: float32 [4608], P('dp'), may hold values from -3 to 3
- local_qkv: float32 [768, 3, 768], P('dp', None, 'mp'), may hold values from -0.21875 to 0.21875
- local_out: float32 [768, 768], P('dp', 'mp'), may hold values from -0.875 to 0.875
- global_qkv: float32 [768, 3, 768], P('dp', None, 'mp'), may hold values from -0.21875 to 0.21875
- global_out: float32 [768, 768], P('dp', 'mp'), may hold values from -0.4375 to 0.4375
- latent_gain: float32 [768], P('dp'), may hold values from 0.1 to 1.9
- up_weight: float32 [768, 3072], P('dp', 'mp'), may hold values from -0.21875 to 0.21875
- down_weight: float32 [768, 3072], P('dp', 'mp'), may hold values from -0.109375 to 0.109375
- group_image: int32 [128], replicated, may hold values from 0 to 7, as said below
- latent_keep: int32 [1024], replicated, may hold values 0 or 1
- token_cotangent: float32 [32768, 768], P('dp'), may hold values from -6 to 6
- latent_cotangent: float32 [1024, 768], P('dp'), may hold values from -6 to 6
Outputs:
- token_output: float32 [32768, 768], P('dp')
- latent_output: float32 [1024, 768], P('dp')
- grad_tokens: float32 [32768, 768], P('dp')
- grad_latents: float32 [1024, 768], P('dp')
- grad_condition: float32 [128, 768], P('dp')
- grad_modulator: float32 [768, 4608], P('dp')
- grad_offsets: float32 [4608], P('dp')
- grad_localqkv: float32 [768, 3, 768], P('dp', None, 'mp')
- grad_localout: float32 [768, 768], P('dp', 'mp')
- grad_globalqkv: float32 [768, 3, 768], P('dp', None, 'mp')
- grad_globalout: float32 [768, 768], P('dp', 'mp')
- grad_gain: float32 [768], P('dp')
- grad_upweight: float32 [768, 3072], P('dp', 'mp')
- grad_downweight: float32 [768, 3072], P('dp', 'mp')
The draws below stay inside these ranges and needn't reach their ends.
Inputs may be any that keep to these rules, and one draw needn't show every extreme that they name: `group_image`: never falling from group to group, starting at 0 and rising by at most one; groups 8 - 1 to 120 always belong to one image.
All inputs are finite; a program needn't handle non-finite values.
Results may differ from the reference program's by a relative error of at most 0.015.
The reference program's roundings to bfloat16 on the way count: a program that leaves them out, or rounds other values in their place, can miss the bound.
Values may be sent and summed in bfloat16 or wider, within the bound.
No kernel may reach another device: no remote copies, remote signals or barrier semaphores. Data moves between devices by JAX's collectives and lax.ppermute only.
A program may use at most 256 MiB of HBM per device.

```python
import math
from functools import partial
import jax
import jax.numpy as jnp
from jax import lax

D = 768
HD = 64
FF = 3072
G_DEV = 8
GROUPS = 128
TOKENS = 32768
LATENTS = 1024


def draw_group_image(key, part):
    key = jax.random.fold_in(key, 11)
    flags = jax.random.randint(key, (GROUPS,), 0, 2)
    number = jnp.arange(GROUPS)
    leading = (number >= 1) & (number < G_DEV) & (flags == 0)
    remaining = G_DEV - 1 - jnp.sum(leading.astype(jnp.int32))
    offset = number - (GROUPS - G_DEV)
    trailing = (offset >= 1) & (offset <= remaining)
    starts = leading | trailing
    return jnp.cumsum(starts.astype(jnp.int32)).astype(jnp.int32)


def with_ends(values, key, low, high):
    index_at = [jax.random.randint(jax.random.fold_in(key, axis), (), 0, length) for axis, length in enumerate(values.shape)]
    longest = values.shape.index(max(values.shape))
    beside = index_at[:longest] + [(index_at[longest] + 1) % values.shape[longest]] + index_at[longest + 1:]
    return values.at[tuple(index_at)].set(low).at[tuple(beside)].set(high)


def shard_levels(own_key, dims, split, least, largest):
    factor_of, own = 1.0, jax.random.fold_in(own_key, 6)
    for dim, shards_of in split:
        steps = jnp.exp(jax.random.uniform(jax.random.fold_in(own, dim), (shards_of,), jnp.float32, least / len(split), largest / len(split)))
        factor_of = factor_of * jnp.repeat(steps, dims[dim] // shards_of).reshape([-1 if axis == dim else 1 for axis in range(len(dims))])
    return factor_of


def scatter_about(own_key, extent, scale, reach, cuts=(), held_as=jnp.bfloat16):
    gain = shard_levels(own_key, extent, cuts, -0.22, 0.18) if cuts else 1.0
    values = jax.random.normal(own_key, extent, jnp.float32) * scale * gain
    return jnp.minimum(jnp.maximum(values, -reach), reach).astype(held_as)


def setup_inputs(seed: int = 0) -> dict:
    splits = jax.random.split(jax.random.key(seed), 17)
    return {
        "tokens": scatter_about(splits[0], (TOKENS, D), 1.0, 6.0, ((0, 16),), jnp.float32),
        "latents": scatter_about(splits[1], (LATENTS, D), 1.0, 6.0, ((0, 16),), jnp.float32),
        "condition": scatter_about(splits[2], (GROUPS, D), 1.0, 6.0, ((0, 16),), jnp.float32),
        "modulator": scatter_about(splits[3], (D, 6 * D), D ** -0.5, 0.21875, ((0, 16),), jnp.float32),
        "offsets": scatter_about(splits[4], (6 * D,), 0.5, 3.0, ((0, 16),), jnp.float32),
        "local_qkv": scatter_about(splits[5], (D, 3, D), D ** -0.5, 0.21875, ((0, 16), (2, 2)), jnp.float32),
        "local_out": scatter_about(splits[6], (D, D), (D // 16) ** -0.5, 0.875, ((0, 16), (1, 2)), jnp.float32),
        "global_qkv": scatter_about(splits[7], (D, 3, D), D ** -0.5, 0.21875, ((0, 16), (2, 2)), jnp.float32),
        "global_out": scatter_about(splits[8], (D, D), (D // 4) ** -0.5, 0.4375, ((0, 16), (1, 2)), jnp.float32),
        "latent_gain": jnp.clip(1.0 + 0.18 * jax.random.normal(splits[9], (D,), jnp.float32), 0.1, 1.9),
        "up_weight": scatter_about(splits[10], (D, FF), D ** -0.5, 0.21875, ((0, 16), (1, 2)), jnp.float32),
        "down_weight": scatter_about(splits[11], (D, FF), FF ** -0.5, 0.109375, ((0, 16), (1, 2)), jnp.float32),
        "group_image": draw_group_image(jax.random.fold_in(splits[16], 71), 0),
        "latent_keep": with_ends((jax.random.randint(splits[13], (LATENTS,), 0, 4) < 3).astype(jnp.int32), jax.random.fold_in(splits[13], 1), 0, 1),
        "token_cotangent": scatter_about(splits[14], (TOKENS, D), 1.0, 6.0, ((0, 16),), jnp.float32),
        "latent_cotangent": scatter_about(splits[15], (LATENTS, D), 1.0, 6.0, ((0, 16),), jnp.float32),
    }


@jax.custom_vjp
def low(v):
    return lax.optimization_barrier(v.astype(jnp.bfloat16)).astype(jnp.float32)

@jax.custom_vjp
def low_back(v):
    return v

def low_keep(v):
    return (low(v), None)

def low_pass(kept, grad):
    return (grad,)

def back_keep(v):
    return (v, None)

def back_low(kept, grad):
    return (low(grad),)
low.defvjp(low_keep, low_pass)
low_back.defvjp(back_keep, back_low)
HIGH = lax.Precision.HIGHEST

def normalize(values):
    center = values - lax.optimization_barrier(jnp.mean(values, -1, keepdims=True))
    return center * lax.rsqrt(lax.optimization_barrier(jnp.mean(center * center, -1, keepdims=True)) + 1e-06)

def local_block(operands):
    queries, key_rows, value_rows = operands
    scores = low_back(jnp.einsum('gnhe,gmhe->ghnm', queries, key_rows, precision=HIGH) * HD ** (-0.5))
    weights = low(jax.nn.softmax(scores, axis=-1))
    return jnp.einsum('ghnm,gmhe->gnhe', weights, value_rows, precision=HIGH)

def forward(group_image, latent_keep, tokens, latents, condition, modulator, offsets, local_qkv, local_out, global_qkv, global_out, latent_gain, up_weight, down_weight):
    groups = condition.shape[0]
    features = tokens.shape[1]
    group_len = tokens.shape[0] // groups
    lat_count = latents.shape[0] // groups
    item_count = group_len + lat_count
    head_count = features // HD
    w_mod, b_mod, w_qkv, w_out, w_gqkv, w_gout, gain_low, w_up, w_down = [low(master) for master in (modulator, offsets, local_qkv, local_out, global_qkv, global_out, latent_gain, up_weight, down_weight)]
    scaled = low(jax.nn.silu(condition))
    modulation = low_back(jnp.dot(scaled, w_mod, precision=HIGH) + b_mod)
    shift_one, scale_one, gate_one, shift_two, scale_two, gate_two = [modulation[:, None, number * features:(number + 1) * features] for number in range(6)]
    items = jnp.concatenate([tokens.reshape(groups, group_len, features), latents.reshape(groups, lat_count, features)], axis=1)
    input_one = low(normalize(items) * (1.0 + scale_one) + shift_one)
    triple = low(low_back(jnp.einsum('gnd,dke->gnke', input_one, w_qkv, precision=HIGH)))
    triple = triple.reshape(groups, item_count, 3, head_count, HD)
    per_step = math.gcd(groups, 16)
    split_qkv = tuple((triple[:, :, number].reshape(groups // per_step, per_step, item_count, head_count, HD) for number in range(3)))
    mixed_heads = lax.map(jax.checkpoint(local_block), split_qkv)
    mixed_heads = low(low_back(mixed_heads.reshape(groups, item_count, features)))
    attended = low_back(jnp.einsum('gnc,dc->gnd', mixed_heads, w_out, precision=HIGH))
    after_local = items + gate_one * attended
    lat_one = after_local[:, group_len:].reshape(groups * lat_count, features)
    lat_input = low(normalize(lat_one) * gain_low)
    lat_triple = low(low_back(jnp.einsum('nd,dke->nke', lat_input, w_gqkv, precision=HIGH)))
    lat_triple = lat_triple.reshape(-1, 3, head_count, HD)
    image_ids = jnp.repeat(group_image, lat_count)
    lat_total = image_ids.shape[0]
    position = jnp.arange(lat_total)
    allowed = (image_ids[:, None] == image_ids[None, :]) & ((latent_keep[None, :] == 1) | (position[:, None] == position[None, :]))
    lat_scores = low_back(jnp.einsum('nhe,mhe->hnm', lat_triple[:, 0], lat_triple[:, 1], precision=HIGH) * HD ** (-0.5))
    lat_scores = jnp.where(allowed[None], lat_scores, -1e+30)
    lat_weights = low(jax.nn.softmax(lat_scores, axis=-1))
    lat_mixed = low(low_back(jnp.einsum('hnm,mhe->nhe', lat_weights, lat_triple[:, 2], precision=HIGH).reshape(lat_total, features)))
    lat_two = lat_one + low_back(jnp.einsum('nc,dc->nd', lat_mixed, w_gout, precision=HIGH))
    after_latent = jnp.concatenate([after_local[:, :group_len], lat_two.reshape(groups, lat_count, features)], axis=1)
    input_two = low(normalize(after_latent) * (1.0 + scale_two) + shift_two)
    upward = low_back(jnp.einsum('gnd,df->gnf', input_two, w_up, precision=HIGH))
    hidden = low(jax.nn.gelu(upward))
    narrowed = low_back(jnp.einsum('gnf,df->gnd', hidden, w_down, precision=HIGH))
    result = after_latent + gate_two * narrowed
    return (result[:, :group_len].reshape(-1, features), result[:, group_len:].reshape(-1, features))

def reference(tokens, latents, condition, modulator, offsets, local_qkv, local_out, global_qkv, global_out, latent_gain, up_weight, down_weight, group_image, latent_keep, token_cotangent, latent_cotangent):
    primals = tuple((master.astype(jnp.float32) for master in (tokens, latents, condition, modulator, offsets, local_qkv, local_out, global_qkv, global_out, latent_gain, up_weight, down_weight)))
    outputs, backward = jax.vjp(partial(forward, group_image, latent_keep), *primals)
    grads = backward((token_cotangent.astype(jnp.float32), latent_cotangent.astype(jnp.float32)))
    return (outputs[0], outputs[1], grads[0], grads[1], grads[2], grads[3], grads[4], grads[5], grads[6], grads[7], grads[8], grads[9], grads[10], grads[11])
```

```python
import jax
import jax.numpy as jnp
from jax import lax
from jax.sharding import PartitionSpec as P

HD = 64
EPSILON = 1e-06
LOWER = jnp.bfloat16
UPPER = jnp.float32


def normalize(values):
    center = values - jnp.mean(values, -1, keepdims=True)
    inverse = lax.rsqrt(jnp.mean(center * center, -1, keepdims=True) + EPSILON)
    return (center * inverse, inverse)


def norm_back(grad_normed, normed, inverse):
    mean_grad = jnp.mean(grad_normed, -1, keepdims=True)
    mean_proj = jnp.mean(grad_normed * normed, -1, keepdims=True)
    return inverse * (grad_normed - mean_grad - normed * mean_proj)


def dot(left, right, dims):
    return lax.dot_general(left, right, ((dims[0], dims[1]), ((), ())), preferred_element_type=UPPER)


def mm(left, right):
    return dot(left, right, ((1,), (0,)))


def mm_nt(left, right):
    return dot(left, right, ((1,), (1,)))


def mm_tn(left, right):
    return dot(left, right, ((0,), (0,)))


class Moves:
    def __init__(self, dp_size):
        self.dp_size = dp_size
        self.staged = dp_size == 16
        self.dp = lax.axis_index("dp")
        self.mp = lax.axis_index("mp")
        if self.staged:
            self.z = self.dp // 4
            self.y = (self.dp // 2) % 2
            self.x = self.dp % 2

    def swap(self, value):
        return lax.ppermute(value, "mp", [(0, 1), (1, 0)])

    def in_order(self, own, other, axis=0):
        return jnp.where(
            self.mp == 0,
            jnp.concatenate([own, other], axis),
            jnp.concatenate([other, own], axis),
        )

    def flip(self, value, bits):
        return lax.ppermute(value, "dp", [(d, d ^ bits) for d in range(16)])

    def turn(self, value, step):
        return lax.ppermute(value, "dp", [(d, (d + 4 * step) % 16) for d in range(16)])

    def pair(self, own, other, index):
        return jnp.where(
            index == 0, jnp.stack([own, other], 1), jnp.stack([other, own], 1)
        )

    def gather(self, value, direct=False):
        if not self.staged:
            return lax.all_gather(value, "dp", axis=0)
        got = [value] + [self.turn(value, step) for step in (1, 2, 3)]
        line = jnp.zeros((4,) + value.shape, value.dtype)
        for step in range(4):
            line = lax.dynamic_update_index_in_dim(line, got[step], (self.z - step) % 4, 0)
        if direct:
            quad = jnp.zeros((4, 4) + value.shape, value.dtype)
            here = self.y * 2 + self.x
            for bits in range(4):
                part = line if bits == 0 else self.flip(line, bits)
                quad = lax.dynamic_update_index_in_dim(quad, part, here ^ bits, 1)
            return quad.reshape((16,) + value.shape)
        first, second = line[:2], line[2:]
        first_x = self.pair(first, self.flip(first, 1), self.x)
        second_y = self.pair(second, self.flip(second, 2), self.y)
        first_all = self.pair(first_x, self.flip(first_x, 2), self.y)
        other = self.flip(second_y, 1)
        second_all = jnp.where(
            self.x == 0, jnp.stack([second_y, other], 2), jnp.stack([other, second_y], 2)
        )
        return jnp.concatenate([first_all, second_all], 0).reshape((16,) + value.shape)

    def pick(self, value, index, axis):
        return lax.dynamic_index_in_dim(value, index, axis, keepdims=False)

    def scatter_sum(self, value):
        if not self.staged:
            return lax.psum_scatter(
                value.astype(UPPER), "dp", scatter_dimension=0, tiled=False
            )
        kind = value.dtype

        def add(one, two):
            return (one.astype(UPPER) + two.astype(UPPER)).astype(kind)

        cube = value.reshape((4, 2, 2) + value.shape[1:])
        first, second = cube[:2], cube[2:]
        got_first = self.flip(self.pick(first, 1 - self.y, 1), 2)
        got_second = self.flip(self.pick(second, 1 - self.x, 2), 1)
        first = add(self.pick(first, self.y, 1), got_first)
        second = add(self.pick(second, self.x, 2), got_second)
        got_first = self.flip(self.pick(first, 1 - self.x, 1), 1)
        got_second = self.flip(self.pick(second, 1 - self.y, 1), 2)
        line = jnp.concatenate(
            [
                add(self.pick(first, self.x, 1), got_first),
                add(self.pick(second, self.y, 1), got_second),
            ],
            0,
        )
        total = self.pick(line, self.z, 0).astype(UPPER)
        for step in (1, 2, 3):
            part = self.pick(line, (self.z + step) % 4, 0)
            total = total + self.turn(part, step).astype(UPPER)
        return total

    def exchange(self, value):
        return lax.all_to_all(value, "dp", 0, 0, tiled=True)


def attention_forward(items, shift, scale, gate, w_qkv, w_out):
    groups, count, features = items.shape
    heads = features // HD
    normed, inverse = normalize(items)
    inputs = (normed * (1.0 + scale) + shift).astype(LOWER)
    triple = jnp.einsum("gnd,dk->gnk", inputs, w_qkv, preferred_element_type=UPPER).astype(LOWER)
    triple = triple.reshape(groups, count, 2, 3, heads // 2, HD)
    queries, keys, values = [
        triple[:, :, :, kind].reshape(groups, count, heads, HD) for kind in range(3)
    ]
    scores = jnp.einsum("gnhe,gmhe->ghnm", queries, keys, preferred_element_type=UPPER) * HD**-0.5
    peak = jnp.max(scores, -1, keepdims=True)
    log_total = peak + jnp.log(jnp.sum(jnp.exp(scores - peak), -1, keepdims=True))
    weights = jnp.exp(scores - log_total)
    mixed = (
        jnp.einsum("ghnm,gmhe->gnhe", weights.astype(LOWER), values, preferred_element_type=UPPER)
        .astype(LOWER)
        .reshape(groups, count, features)
    )
    attended = jnp.einsum("gnc,dc->gnd", mixed, w_out, preferred_element_type=UPPER)
    after = items + gate * attended
    return after, (normed, inverse, inputs, queries, keys, values, log_total, mixed, attended)


def attention_backward(grad_after, saved, scale, gate, w_qkv, w_out):
    normed, inverse, inputs, queries, keys, values, log_total, mixed, attended = saved
    groups, count, features = normed.shape
    heads = features // HD
    grad_gate = jnp.sum(grad_after * attended, 1)
    grad_attended = (gate * grad_after).astype(LOWER)
    out_grad = jnp.einsum("gnd,gnc->dc", grad_attended, mixed, preferred_element_type=UPPER)
    grad_mixed = (
        jnp.einsum("gnd,dc->gnc", grad_attended, w_out, preferred_element_type=UPPER)
        .astype(LOWER)
        .reshape(groups, count, heads, HD)
    )
    scores = jnp.einsum("gnhe,gmhe->ghnm", queries, keys, preferred_element_type=UPPER) * HD**-0.5
    weights = jnp.exp(scores - log_total)
    grad_weights = jnp.einsum("gnhe,gmhe->ghnm", grad_mixed, values, preferred_element_type=UPPER)
    delta = jnp.sum(grad_weights * weights, -1, keepdims=True)
    grad_scores = (weights * (grad_weights - delta)).astype(LOWER)
    grad_queries = (
        jnp.einsum("ghnm,gmhe->gnhe", grad_scores, keys, preferred_element_type=UPPER) * HD**-0.5
    ).astype(LOWER)
    grad_keys = (
        jnp.einsum("ghnm,gnhe->gmhe", grad_scores, queries, preferred_element_type=UPPER) * HD**-0.5
    ).astype(LOWER)
    grad_values = jnp.einsum(
        "ghnm,gnhe->gmhe", weights.astype(LOWER), grad_mixed, preferred_element_type=UPPER
    ).astype(LOWER)
    grad_triple = jnp.stack(
        [
            part.reshape(groups, count, 2, heads // 2, HD)
            for part in (grad_queries, grad_keys, grad_values)
        ],
        axis=3,
    ).reshape(groups, count, 3 * features)
    qkv_grad = jnp.einsum("gnd,gnk->dk", inputs, grad_triple, preferred_element_type=UPPER)
    grad_inputs = jnp.einsum("gnk,dk->gnd", grad_triple, w_qkv, preferred_element_type=UPPER)
    grad_shift = jnp.sum(grad_inputs, 1)
    grad_scale = jnp.sum(grad_inputs * normed, 1)
    grad_items = grad_after + norm_back(grad_inputs * (1.0 + scale), normed, inverse)
    return grad_items, grad_shift, grad_scale, grad_gate, qkv_grad, out_grad


def feed_forward(rows, grad_result, shift, scale, gate, w_up, w_down):
    normed, inverse = normalize(rows)
    inputs = (normed * (1.0 + scale) + shift).astype(LOWER)
    upward = jnp.einsum("gnd,df->gnf", inputs, w_up, preferred_element_type=UPPER)
    hidden, pull = jax.vjp(jax.nn.gelu, upward)
    hidden = hidden.astype(LOWER)
    narrowed = jnp.einsum("gnf,df->gnd", hidden, w_down, preferred_element_type=UPPER)
    result = rows + gate * narrowed
    grad_gate = jnp.sum(grad_result * narrowed, 1)
    grad_narrow = (gate * grad_result).astype(LOWER)
    grad_hidden = jnp.einsum("gnd,df->gnf", grad_narrow, w_down, preferred_element_type=UPPER)
    grad_upward = pull(grad_hidden)[0].astype(LOWER)
    down_grad = jnp.einsum("gnd,gnf->df", grad_narrow, hidden, preferred_element_type=UPPER)
    up_grad = jnp.einsum("gnd,gnf->df", inputs, grad_upward, preferred_element_type=UPPER)
    grad_inputs = jnp.einsum("gnf,df->gnd", grad_upward, w_up, preferred_element_type=UPPER)
    grad_shift = jnp.sum(grad_inputs, 1)
    grad_scale = jnp.sum(grad_inputs * normed, 1)
    grad_rows = grad_result + norm_back(grad_inputs * (1.0 + scale), normed, inverse)
    return result, grad_rows, grad_shift, grad_scale, grad_gate, up_grad, down_grad


def split_three(value):
    high = lax.reduce_precision(value, 8, 7)
    rest = value - high
    middle = lax.reduce_precision(rest, 8, 7)
    return [part.astype(LOWER) for part in (high, middle, rest - middle)]


def make_body(dp_size):
    def body(
        tokens,
        latents,
        condition,
        modulator,
        offsets,
        local_qkv,
        local_out,
        global_qkv,
        global_out,
        latent_gain,
        up_weight,
        down_weight,
        group_image,
        latent_keep,
        token_cotangent,
        latent_cotangent,
    ):
        move = Moves(dp_size)
        mp = move.mp
        groups = condition.shape[0]
        own = groups // 2
        features = tokens.shape[1]
        group_len = tokens.shape[0] // groups
        lat_count = latents.shape[0] // groups
        shard = modulator.shape[0]
        half = local_out.shape[1]
        units = up_weight.shape[1]
        width = modulator.shape[1]
        heads = half // HD

        def mine(value, axis=0):
            size = value.shape[axis] // 2
            return lax.dynamic_slice_in_dim(value, mp * size, size, axis)

        def others(value, axis=0):
            size = value.shape[axis] // 2
            return lax.dynamic_slice_in_dim(value, (1 - mp) * size, size, axis)

        scaled = jax.nn.silu(condition).astype(LOWER)
        extra = jnp.concatenate([latent_gain, offsets]).astype(LOWER)
        extra = jnp.pad(extra, (0, features - extra.shape[0]))[None]
        vectors = move.gather(jnp.concatenate([scaled, extra], 0), direct=True)
        scaled_all = vectors[:, :groups].reshape(dp_size * groups, features)
        gain = vectors[:, groups, :shard].reshape(features).astype(UPPER)
        bias = vectors[:, groups, shard : shard + width // dp_size].reshape(width).astype(UPPER)
        scaled_mine = lax.dynamic_slice_in_dim(scaled_all, move.dp * shard, shard, 1)

        def modulate(columns, bias_part):
            terms = mm(scaled_mine, mine(columns, 1).astype(LOWER))
            total = move.scatter_sum(terms.reshape(dp_size, groups, -1))
            full = move.in_order(mine(total), move.swap(others(total)), 1)
            return [
                part[:, None] for part in jnp.split(full + bias_part[None], 3, axis=1)
            ]

        middle = width // 2
        shift_one, scale_one, gate_one = modulate(modulator[:, :middle], bias[:middle])

        def whole(shard_rows, direct=False):
            gathered = move.gather(shard_rows, direct)
            return gathered.reshape((features,) + shard_rows.shape[1:])

        qkv_mine = whole(local_qkv.reshape(shard, 3 * half).astype(LOWER))
        w_qkv = jnp.concatenate([qkv_mine, move.swap(qkv_mine)], 1)
        small = whole(
            jnp.concatenate(
                [local_out, global_qkv.reshape(shard, 3 * half), global_out], 1
            ).astype(LOWER)
        )
        out_mine = small[:, :half]
        w_gqkv = small[:, half : 4 * half]
        w_gout = small[:, 4 * half :]
        w_out = jnp.concatenate([out_mine, move.swap(out_mine)], 1)
        wide = whole(jnp.concatenate([up_weight, down_weight], 1).astype(LOWER))
        wide_other = move.swap(wide)
        w_up = jnp.concatenate([wide[:, :units], wide_other[:, :units]], 1)
        w_down = jnp.concatenate([wide[:, units:], wide_other[:, units:]], 1)
        shift_two, scale_two, gate_two = modulate(modulator[:, middle:], bias[middle:])

        own_tokens = mine(tokens).reshape(own, group_len, features)
        own_latents = mine(latents).reshape(own, lat_count, features)
        items = jnp.concatenate([own_tokens, own_latents], axis=1)
        after_local, saved = attention_forward(
            items, shift_one, scale_one, gate_one, w_qkv, w_out
        )
        lat_one = after_local[:, group_len:].reshape(own * lat_count, features)

        lat_normed, lat_inverse = normalize(lat_one)
        lat_input = (lat_normed * gain).astype(LOWER)
        lat_input = move.in_order(lat_input, move.swap(lat_input))
        lat_triple = mm(lat_input, w_gqkv).astype(LOWER)
        chip_count = groups * lat_count
        lat_total = dp_size * chip_count
        key_values = move.gather(lat_triple[:, half:], direct=True).reshape(lat_total, 2 * half)

        def by_head(value):
            return value.reshape(value.shape[0], heads, HD)

        lat_queries = by_head(lat_triple[:, :half])
        key_heads, value_heads = by_head(key_values[:, :half]), by_head(key_values[:, half:])
        images = jnp.repeat(group_image, lat_count)
        first = move.dp * chip_count
        own_images = lax.dynamic_slice_in_dim(images, first, chip_count)
        own_keep = lax.dynamic_slice_in_dim(latent_keep, first, chip_count)
        rows = first + jnp.arange(chip_count)
        same = (own_images[:, None] == images[None, :])
        itself = rows[:, None] == jnp.arange(lat_total)[None, :]
        allowed = same & ((latent_keep[None, :] == 1) | itself)
        allowed_keys = same & ((own_keep[:, None] == 1) | itself)
        lat_scores = (
            jnp.einsum("nhe,mhe->hnm", lat_queries, key_heads, preferred_element_type=UPPER)
            * HD**-0.5
        )
        lat_scores = jnp.where(allowed[None], lat_scores, -1e30)
        lat_peak = jnp.max(lat_scores, -1, keepdims=True)
        lat_log = lat_peak + jnp.log(jnp.sum(jnp.exp(lat_scores - lat_peak), -1, keepdims=True))
        lat_weights = jnp.exp(lat_scores - lat_log)
        lat_mixed = (
            jnp.einsum(
                "hnm,mhe->nhe", lat_weights.astype(LOWER), value_heads, preferred_element_type=UPPER
            )
            .astype(LOWER)
            .reshape(chip_count, half)
        )
        branch = mm_nt(lat_mixed, w_gout)
        branch = mine(branch) + move.swap(others(branch))
        lat_two = lat_one + branch

        token_grad = mine(token_cotangent).reshape(own, group_len, features)
        lat_grad = mine(latent_cotangent).reshape(own, lat_count, features)
        (
            token_result,
            grad_tokens_two,
            shift_a,
            scale_a,
            gate_a,
            up_a,
            down_a,
        ) = feed_forward(
            after_local[:, :group_len], token_grad, shift_two, scale_two, gate_two, w_up, w_down
        )
        (
            lat_result,
            grad_lat_two,
            shift_b,
            scale_b,
            gate_b,
            up_b,
            down_b,
        ) = feed_forward(
            lat_two.reshape(own, lat_count, features),
            lat_grad,
            shift_two,
            scale_two,
            gate_two,
            w_up,
            w_down,
        )
        grad_shift_two, grad_scale_two, grad_gate_two = (
            shift_a + shift_b,
            scale_a + scale_b,
            gate_a + gate_b,
        )

        def reduce(value_mine, value_other):
            both = (value_mine + move.swap(value_other.astype(LOWER)).astype(UPPER)).astype(LOWER)
            return move.scatter_sum(both.reshape(dp_size, shard, -1))

        up_grad, down_grad = (up_a + up_b), (down_a + down_b)
        wide_grad = reduce(
            jnp.concatenate([up_grad[:, :units], down_grad[:, :units]], 1),
            jnp.concatenate([up_grad[:, units:], down_grad[:, units:]], 1),
        )
        token_output = move.in_order(token_result, move.swap(token_result))
        latent_output = move.in_order(lat_result, move.swap(lat_result))

        grad_lat_two = grad_lat_two.reshape(own * lat_count, features)
        grad_branch = grad_lat_two.astype(LOWER)
        grad_branch = move.in_order(grad_branch, move.swap(grad_branch))
        grad_mixed_rows = mm(grad_branch, w_gout).astype(LOWER)
        grad_mixed = by_head(grad_mixed_rows)
        gout_grad = mm_tn(grad_branch, lat_mixed)
        grad_weights = jnp.einsum(
            "nhe,mhe->hnm", grad_mixed, value_heads, preferred_element_type=UPPER
        )
        delta = jnp.sum(grad_weights * lat_weights, -1, keepdims=True)
        grad_scores = (lat_weights * (grad_weights - delta)).astype(LOWER)
        grad_queries = (
            jnp.einsum("hnm,mhe->nhe", grad_scores, key_heads, preferred_element_type=UPPER)
            * HD**-0.5
        ).astype(LOWER)
        stats = split_three(lat_log[..., 0].T) + split_three(delta[..., 0].T)
        stats = jnp.pad(jnp.concatenate(stats, 1), ((0, 0), (0, 128 - 6 * heads)))
        sent = jnp.concatenate([lat_triple[:, :half], grad_mixed_rows, stats], 1)
        came = move.gather(sent, direct=True).reshape(lat_total, -1)
        all_queries, all_grads = by_head(came[:, :half]), by_head(came[:, half : 2 * half])
        parts = came[:, 2 * half :].astype(UPPER)

        def rejoin(at):
            return sum(
                parts[:, (at + number) * heads : (at + number + 1) * heads] for number in range(3)
            ).T[:, None, :]

        all_log, all_delta = rejoin(0), rejoin(3)
        own_keys, own_values = by_head(lat_triple[:, half : 2 * half]), by_head(
            lat_triple[:, 2 * half :]
        )
        back_scores = (
            jnp.einsum("mhe,nhe->hmn", own_keys, all_queries, preferred_element_type=UPPER)
            * HD**-0.5
        )
        back_weights = jnp.exp(jnp.where(allowed_keys[None], back_scores - all_log, -1e30))
        back_grads = jnp.einsum(
            "mhe,nhe->hmn", own_values, all_grads, preferred_element_type=UPPER
        )
        back_scores_grad = (back_weights * (back_grads - all_delta)).astype(LOWER)
        grad_keys = (
            jnp.einsum("hmn,nhe->mhe", back_scores_grad, all_queries, preferred_element_type=UPPER)
            * HD**-0.5
        ).astype(LOWER)
        grad_values = jnp.einsum(
            "hmn,nhe->mhe", back_weights.astype(LOWER), all_grads, preferred_element_type=UPPER
        ).astype(LOWER)
        grad_lat_triple = jnp.concatenate(
            [part.reshape(chip_count, half) for part in (grad_queries, grad_keys, grad_values)], 1
        )
        gqkv_grad = mm_tn(lat_input, grad_lat_triple)
        grad_lat_input = mm_nt(grad_lat_triple, w_gqkv)
        grad_lat_input = mine(grad_lat_input) + move.swap(others(grad_lat_input))
        gain_part = jnp.sum(grad_lat_input * lat_normed, 0)
        grad_lat_one = grad_lat_two + norm_back(grad_lat_input * gain, lat_normed, lat_inverse)

        grad_after = jnp.concatenate(
            [grad_tokens_two, grad_lat_one.reshape(own, lat_count, features)], axis=1
        )
        grad_items, grad_shift_one, grad_scale_one, grad_gate_one, qkv_grad, out_grad = (
            attention_backward(grad_after, saved, scale_one, gate_one, w_qkv, w_out)
        )
        out_both = out_grad[:, :half] + move.swap(out_grad[:, half:].astype(LOWER)).astype(UPPER)
        small_grad = move.scatter_sum(
            jnp.concatenate([out_both, gqkv_grad, gout_grad], 1)
            .astype(LOWER)
            .reshape(dp_size, shard, -1)
        )
        qkv_sum = reduce(qkv_grad[:, : 3 * half], qkv_grad[:, 3 * half :])
        grad_tokens = grad_items[:, :group_len]
        grad_tokens = move.in_order(grad_tokens, move.swap(grad_tokens))
        grad_latents = grad_items[:, group_len:]
        grad_latents = move.in_order(grad_latents, move.swap(grad_latents))

        grad_modulation = jnp.concatenate(
            [
                grad_shift_one,
                grad_scale_one,
                grad_gate_one,
                grad_shift_two,
                grad_scale_two,
                grad_gate_two,
            ],
            axis=-1,
        ).astype(LOWER)
        gain_row = jnp.pad(
            jnp.concatenate(split_three(gain_part)), (0, width - 3 * features)
        )[None]
        rows_sent = jnp.concatenate([grad_modulation, gain_row], 0)
        rows_all = move.gather(rows_sent, direct=True)
        rows_other = move.swap(rows_all)
        gain_all = (rows_all[:, own].astype(UPPER) + rows_other[:, own].astype(UPPER)).sum(0)
        gain_all = gain_all[: 3 * features].reshape(3, features).sum(0)
        gain_grad = lax.dynamic_slice_in_dim(gain_all, move.dp * shard, shard)
        mod_all = move.in_order(rows_all[:, :own], rows_other[:, :own], 1).reshape(-1, width)
        mod_grad = mm_tn(scaled_mine, mod_all)
        bias_all = jnp.sum(mod_all.astype(UPPER), 0)
        piece = width // dp_size
        bias_grad = lax.dynamic_slice_in_dim(bias_all, move.dp * piece, piece)
        grad_scaled = mm_nt(mod_all, modulator.astype(LOWER)).reshape(dp_size, groups, shard)
        grad_scaled = move.exchange(grad_scaled).transpose(1, 0, 2).reshape(groups, features)
        grad_condition = jax.vjp(jax.nn.silu, condition)[1](grad_scaled)[0]

        return (
            token_output.reshape(-1, features),
            latent_output.reshape(-1, features),
            grad_tokens.reshape(-1, features),
            grad_latents.reshape(-1, features),
            grad_condition,
            mod_grad,
            bias_grad,
            qkv_sum.reshape(shard, 3, half),
            small_grad[:, :half],
            small_grad[:, half : 4 * half].reshape(shard, 3, half),
            small_grad[:, 4 * half :],
            gain_grad,
            wide_grad[:, :units],
            wide_grad[:, units:],
        )

    return body


def solution(mesh):
    rows, heads = P("dp", None), P("dp", None, "mp")
    columns, vector = P("dp", "mp"), P("dp")
    return jax.shard_map(
        make_body(mesh.shape["dp"]),
        mesh=mesh,
        in_specs=(
            rows,
            rows,
            rows,
            rows,
            vector,
            heads,
            columns,
            heads,
            columns,
            vector,
            columns,
            columns,
            P(),
            P(),
            rows,
            rows,
        ),
        out_specs=(
            rows,
            rows,
            rows,
            rows,
            rows,
            rows,
            vector,
            heads,
            columns,
            heads,
            columns,
            vector,
            columns,
            columns,
        ),
        check_vma=False,
    )
```

```python
import jax
import jax.numpy as jnp
from jax import lax
from jax.experimental import pallas as pl
from jax.experimental.pallas import tpu as pltpu
from jax.sharding import PartitionSpec as P

HD = 64
EPSILON = 1e-06
SCALING = HD**-0.5
LOWER = jnp.bfloat16
UPPER = jnp.float32
NEVER = -1e30
SLOT = 16
VMEM_LIMIT = 56 * 1024 * 1024


def dot(left, right, dims):
    return lax.dot_general(left, right, ((dims[0], dims[1]), ((), ())), preferred_element_type=UPPER)


def mm(left, right):
    return dot(left, right, ((1,), (0,)))


def mm_nt(left, right):
    return dot(left, right, ((1,), (1,)))


def mm_tn(left, right):
    return dot(left, right, ((0,), (0,)))


def normalize(values):
    center = values - jnp.mean(values, -1, keepdims=True)
    inverse = lax.rsqrt(jnp.mean(center * center, -1, keepdims=True) + EPSILON)
    return (center * inverse, inverse)


def norm_back(grad_normed, normed, inverse):
    mean_grad = jnp.mean(grad_normed, -1, keepdims=True)
    mean_proj = jnp.mean(grad_normed * normed, -1, keepdims=True)
    return inverse * (grad_normed - mean_grad - normed * mean_proj)


class Moves:
    def __init__(self, dp_size):
        self.dp_size = dp_size
        self.staged = dp_size == 16
        self.dp = lax.axis_index("dp")
        self.mp = lax.axis_index("mp")
        if self.staged:
            self.blocks = (4, 4)
            z, here = self.dp // 4, self.dp % 4
            came = [((z - k) % 4) * 4 + (here ^ b) for b in range(4) for k in range(4)]
            goes = [((z + k) % 4) * 4 + (here ^ b) for b in range(4) for k in range(4)]
        else:
            self.blocks = (1, 1)
            came = goes = [self.dp * 0]
        self.came_at, self.goes_at, self.chips_at = 2, 2 + len(came), 2
        table = [self.mp, self.dp] + came + goes
        if not self.staged:
            self.chips_at = len(table)
            table += [self.dp * 0 + chip for chip in range(dp_size)]
        self.info = jnp.stack(table).astype(jnp.int32)

    def swap(self, value):
        return lax.ppermute(value, "mp", [(0, 1), (1, 0)])

    def in_order(self, own, other, axis=0):
        return jnp.where(
            self.mp == 0,
            jnp.concatenate([own, other], axis),
            jnp.concatenate([other, own], axis),
        )

    def flip(self, value, bits):
        return lax.ppermute(value, "dp", [(d, d ^ bits) for d in range(16)])

    def turn(self, value, step):
        return lax.ppermute(value, "dp", [(d, (d + 4 * step) % 16) for d in range(16)])

    def line(self, value):
        if not self.staged:
            return value
        return jnp.stack([value] + [self.turn(value, step) for step in (1, 2, 3)])

    def spread(self, line, chips=False):
        if not self.staged:
            value = lax.all_gather(line, "dp", axis=0, tiled=not chips)
            return [value if chips else value[None]]
        return [line] + [self.flip(line, bits) for bits in (1, 2, 3)]

    def meet(self, parts):
        if not self.staged:
            return parts
        return [parts[0]] + [self.flip(parts[bits], bits) for bits in (1, 2, 3)]

    def fold(self, terms):
        if not self.staged:
            return terms
        size = terms[0].shape[0] // 4
        sums = [
            sum(term[step * size : (step + 1) * size].astype(UPPER) for term in terms)
            for step in range(4)
        ]
        return sums[:1] + [part.astype(terms[0].dtype) for part in sums[1:]]

    def finish(self, sums):
        if not self.staged:
            return lax.psum_scatter(
                sums[0].astype(UPPER), "dp", scatter_dimension=0, tiled=True
            )
        total = sums[0]
        for step in (1, 2, 3):
            total = total + self.turn(sums[step], step).astype(UPPER)
        return total

    def square_to_line(self, value):
        if not self.staged:
            return value
        rows, columns = value.shape
        groups = [[4 * z + here for here in range(4)] for z in range(4)]
        value = lax.all_to_all(
            value.reshape(4, rows // 4, columns), "dp", 0, 0, axis_index_groups=groups, tiled=True
        )
        total = sum(value[number].astype(UPPER) for number in range(4)).astype(value.dtype)
        return total.reshape(4, rows // 16, columns)

    def line_to_own(self, value):
        if not self.staged:
            return lax.psum_scatter(value.astype(UPPER), "dp", scatter_dimension=0, tiled=True)
        groups = [[4 * z + here for z in range(4)] for here in range(4)]
        value = lax.all_to_all(value, "dp", 0, 0, axis_index_groups=groups, tiled=True)
        return sum(value[number].astype(UPPER) for number in range(4))

    def sum_cores(self, parts, other):
        came = self.swap(other)
        size = parts[0].shape[0]
        return [
            (part.astype(UPPER) + came[b * size : (b + 1) * size].astype(UPPER)).astype(LOWER)
            for b, part in enumerate(parts)
        ]


def wait_for(value, *others):
    return lax.optimization_barrier((value, *others))[0]


ANY = pl.BlockSpec(memory_space=pl.ANY)


def whole(shape):
    return pl.BlockSpec(shape, lambda *_: (0,) * len(shape))


def call(kernel, info, inputs, outputs, scratch=(), grid=(1,), flops=0, moved=0, name=None, after=(), aliased=()):
    skipped = list(aliased) + list(after)

    def inner(info_ref, *refs):
        kernel(info_ref, *refs[len(skipped) :])

    inputs = [(array, ANY) for array in skipped] + inputs
    return pl.pallas_call(
        inner,
        input_output_aliases={1 + number: number for number in range(len(aliased))},
        out_shape=[jax.ShapeDtypeStruct(shape, kind) for shape, kind, _ in outputs],
        grid_spec=pltpu.PrefetchScalarGridSpec(
            num_scalar_prefetch=1,
            grid=grid,
            in_specs=[spec for _, spec in inputs],
            out_specs=[spec for _, _, spec in outputs],
            scratch_shapes=list(scratch),
        ),
        compiler_params=pltpu.CompilerParams(
            dimension_semantics=("arbitrary",) * len(grid), vmem_limit_bytes=VMEM_LIMIT
        ),
        cost_estimate=pl.CostEstimate(flops=flops, bytes_accessed=moved, transcendentals=0),
        name=name,
    )(info, *[array for array, _ in inputs])


def bring(info, at, pieces, parts, sems, take=None):
    copies = []
    for b, piece in enumerate(pieces):
        count, rows, _ = piece.shape
        rows = take or rows
        for k in range(count):
            number = b * count + k
            start = pl.multiple_of(info[at + number] * rows, 16)
            for p, (target, column, source, columns) in enumerate(parts):
                copy = pltpu.make_async_copy(
                    piece.at[k, pl.ds(0, rows), pl.ds(source, columns)],
                    target.at[pl.ds(start, rows), pl.ds(column, columns)],
                    sems.at[number * len(parts) + p],
                )
                copy.start()
                copies.append(copy)
    return copies


def place(info, at, full, targets, column, columns, single=False):
    if single:
        (target,) = targets
    nb, nk = (4, 4) if at > 3 else (1, 1)
    rows = full.shape[0] // (nb * nk)
    for b in range(nb):
        for k in range(nk):
            start = pl.multiple_of(info[at + b * nk + k] * rows, 16)
            value = full[pl.ds(start, rows), :]
            if single:
                target[(b * nk + k) * rows : (b * nk + k + 1) * rows, column : column + columns] = value
            else:
                targets[b][k * rows : (k + 1) * rows, column : column + columns] = value


def place_square(staged, full, target, column, columns):
    if not staged:
        target[:, column : column + columns] = full[...]
        return
    rows = full.shape[0] // 16
    for here in range(4):
        for z in range(4):
            target[(here * 4 + z) * rows : (here * 4 + z + 1) * rows, column : column + columns] = full[
                (z * 4 + here) * rows : (z * 4 + here + 1) * rows, :
            ]


def grouped_rows(tokens, latents):
    pad = jnp.zeros((SLOT - latents.shape[0], latents.shape[1]), UPPER)
    return jnp.concatenate([tokens, latents, pad], 0)


def attention_forward(move, first, count, tokens, latents, mod, own_w, other_w, sizes):
    group_len, lat_count, features, half = sizes
    groups = tokens.shape[0] // group_len
    length = group_len + SLOT
    real = group_len + lat_count
    heads = half // HD
    np_ = len(own_w)

    def kernel(info, tok, lat, mod_ref, *refs):
        own, other = refs[:np_], refs[np_ : 2 * np_]
        after, lat_one, triple_ref, stats, mixed_ref, att_ref = refs[2 * np_ : 2 * np_ + 6]
        w_own, w_other, w_out, sems = refs[2 * np_ + 6 :]

        @pl.when(pl.program_id(0) == 0)
        def _():
            number = sems.shape[0] // 2
            copies = bring(
                info, move.came_at, own,
                [(w_own, 0, 0, 3 * half), (w_out, 0, 3 * half, half)], sems.at[pl.ds(0, number)],
            ) + bring(
                info, move.came_at, other,
                [(w_other, 0, 0, 3 * half), (w_out, half, 3 * half, half)],
                sems.at[pl.ds(number, number)],
            )
            for copy in copies:
                copy.wait()

        rows = grouped_rows(tok[...], lat[...])
        shift, scale, gate = [mod_ref[0, :, i * features : (i + 1) * features] for i in range(3)]
        normed, _ = normalize(rows)
        inputs = (normed * (1.0 + scale) + shift).astype(LOWER)
        for side, weight in ((0, w_own), (1, w_other)):
            triple = mm(inputs, weight[...]).astype(LOWER)
            triple_ref[:, side * 3 * half : (side + 1) * 3 * half] = triple
            pair = []
            for head in range(heads):
                query, key, value = [
                    triple[:, kind * half + head * HD : kind * half + (head + 1) * HD]
                    for kind in range(3)
                ]
                scores = mm_nt(key, query) * SCALING
                scores = jnp.concatenate(
                    [scores[:real], jnp.full((length - real, length), NEVER, UPPER)], 0
                )
                peak = jnp.max(scores, 0, keepdims=True)
                weights = jnp.exp(scores - peak)
                total = jnp.sum(weights, 0, keepdims=True)
                stats[0, side * heads + head : side * heads + head + 1, :] = peak + jnp.log(total)
                weights = (weights * (1.0 / total)).astype(LOWER)
                pair.append(mm_tn(weights, value).astype(LOWER))
                if len(pair) == 2:
                    at = side * half + (head - 1) * HD
                    mixed_ref[:, at : at + 2 * HD] = jnp.concatenate(pair, 1)
                    pair = []
        attended = mm_nt(mixed_ref[...], w_out[...])
        att_ref[...] = attended.astype(LOWER)
        result = rows + gate * attended
        after[...] = result[:group_len]
        lat_one[...] = result[group_len:real]

    at = lambda g, info: (info[0] * groups // 2 + first + g, 0)
    sems = 2 * np_ * own_w[0].shape[0]
    return call(
        kernel,
        move.info,
        [
            (tokens, pl.BlockSpec((group_len, features), at)),
            (latents, pl.BlockSpec((lat_count, features), at)),
            (mod, pl.BlockSpec((1, 1, 3 * features), lambda g, info: (first + g, 0, 0))),
        ]
        + [(piece, ANY) for piece in own_w + other_w],
        [
            ((count * group_len, features), UPPER, pl.BlockSpec((group_len, features), lambda g, info: (g, 0))),
            ((count * lat_count, features), UPPER, pl.BlockSpec((lat_count, features), lambda g, info: (g, 0))),
            ((count * length, 6 * half), LOWER, pl.BlockSpec((length, 6 * half), lambda g, info: (g, 0))),
            ((count, 2 * heads, length), UPPER, pl.BlockSpec((1, 2 * heads, length), lambda g, info: (g, 0, 0))),
            ((count * length, features), LOWER, pl.BlockSpec((length, features), lambda g, info: (g, 0))),
            ((count * length, features), LOWER, pl.BlockSpec((length, features), lambda g, info: (g, 0))),
        ],
        [
            pltpu.VMEM((features, 3 * half), LOWER),
            pltpu.VMEM((features, 3 * half), LOWER),
            pltpu.VMEM((features, 2 * half), LOWER),
            pltpu.SemaphoreType.DMA((2 * sems,)),
        ],
        grid=(count,),
        flops=count * length * features * features * 8 * 2,
        moved=count * 4_000_000,
        name="attention_forward",
    )


def attention_entry(
    move, lat_own, lat_came, lat_one, grad_two, gain, mod, grad_tok, attended, sizes, after=()
):
    group_len, lat_count, features, half = sizes
    count = lat_one.shape[0] // lat_count
    length = group_len + SLOT

    def kernel(info, own, came, lat, two, gain_ref, mod_ref, gtok, att, grad_lat, grad_att, vec):
        normed, inverse = normalize(lat[...])
        into = two[...] + norm_back((own[...] + came[...]) * gain_ref[...], normed, inverse)
        grad_lat[...] = into
        rows = grouped_rows(gtok[...], into)
        vec[0] = jnp.sum(rows * att[...].astype(UPPER), 0, keepdims=True)
        grad_att[...] = (mod_ref[0, :, 2 * features :] * rows).astype(LOWER)

    row = lambda size, columns: pl.BlockSpec((size, columns), lambda g, info: (g, 0))
    return call(
        kernel,
        move.info,
        [(value, row(lat_count, features)) for value in (lat_own, lat_came, lat_one, grad_two)]
        + [
            (gain, whole(gain.shape)),
            (mod, pl.BlockSpec((1, 1, 3 * features), lambda g, info: (g, 0, 0))),
            (grad_tok, row(group_len, features)),
            (attended, row(length, features)),
        ],
        [
            ((count * lat_count, features), UPPER, row(lat_count, features)),
            ((count * length, features), LOWER, row(length, features)),
            ((count, 1, features), UPPER, pl.BlockSpec((1, 1, features), lambda g, info: (g, 0, 0))),
        ],
        grid=(count,),
        flops=count * length * features * 10,
        moved=count * 2_500_000,
        name="attention_entry",
        after=after,
    )


def attention_backward(
    move, first, count, tokens, latents, mod, grad_tok, grad_lat, grad_att, saved, own_w, other_w, sizes, before=(), after=()
):
    group_len, lat_count, features, half = sizes
    groups = tokens.shape[0] // group_len
    mine = groups // 2
    length = group_len + SLOT
    real = group_len + lat_count
    heads = half // HD
    np_ = len(own_w)
    triple_all, stats_all = saved

    def kernel(info, tok, lat, mod_ref, gtok, glat, gatt, triple, stats, *refs):
        own, other = refs[:np_], refs[np_ : 2 * np_]
        out_tok, out_lat, in_ref, tri_ref, vec_ref, full = refs[2 * np_ : 2 * np_ + 6]
        w_in, w_out, sems = refs[2 * np_ + 6 :]

        @pl.when(pl.program_id(0) == 0)
        def _():
            number = sems.shape[0] // 2
            copies = []
            for side, pieces in ((0, own), (1, other)):
                parts = [(w_in, side * 3 * half, 0, 3 * half), (w_out, side * half, 3 * half, half)]
                copies += bring(info, move.came_at, pieces, parts, sems.at[pl.ds(side * number, number)])
            for copy in copies:
                copy.wait()

        rows = grouped_rows(tok[...], lat[...])
        shift, scale = [mod_ref[0, :, i * features : (i + 1) * features] for i in range(2)]
        normed, inverse = normalize(rows)
        in_ref[...] = (normed * (1.0 + scale) + shift).astype(LOWER)
        grad_mixed_all = mm(gatt[...], w_out[...]).astype(LOWER)
        for side in range(2):
            pairs = ([], [], [])
            for head in range(heads):
                base = side * 3 * half + head * HD
                query, key, value = [
                    triple[:, base + kind * half : base + kind * half + HD] for kind in range(3)
                ]
                at = side * half + head * HD
                grad_mixed = grad_mixed_all[:, at : at + HD]
                scores = mm_nt(key, query) * SCALING
                scores = jnp.concatenate(
                    [scores[:real], jnp.full((length - real, length), NEVER, UPPER)], 0
                )
                weights = jnp.exp(scores - stats[0, side * heads + head : side * heads + head + 1, :])
                grad_weights = mm_nt(value, grad_mixed)
                delta = jnp.sum(grad_weights * weights, 0, keepdims=True)
                grad_scores = (weights * (grad_weights - delta)).astype(LOWER)
                pairs[0].append((mm_tn(grad_scores, key) * SCALING).astype(LOWER))
                pairs[1].append((mm(grad_scores, query) * SCALING).astype(LOWER))
                pairs[2].append(mm(weights.astype(LOWER), grad_mixed).astype(LOWER))
                if head % 2:
                    for kind in range(3):
                        at = base + kind * half - HD
                        tri_ref[:, at : at + 2 * HD] = jnp.concatenate(pairs[kind][-2:], 1)
        grad_inputs = mm_nt(tri_ref[...], w_in[...])
        vec_ref[0, 0:1, :] = jnp.sum(grad_inputs, 0, keepdims=True)
        vec_ref[0, 1:2, :] = jnp.sum(grad_inputs * normed, 0, keepdims=True)
        result = grouped_rows(gtok[...], glat[...]) + norm_back(
            grad_inputs * (1.0 + scale), normed, inverse
        )
        out_tok[...] = result[:group_len]
        full[...] = result[:group_len]
        out_lat[...] = result[group_len:real]

    at = lambda g, info: (info[0] * mine + first + g, 0)
    row = lambda size, columns: pl.BlockSpec((size, columns), lambda g, info: (first + g, 0))
    vector = lambda n, size: pl.BlockSpec((1, n, size), lambda g, info: (first + g, 0, 0))
    return call(
        kernel,
        move.info,
        [
            (tokens, pl.BlockSpec((group_len, features), at)),
            (latents, pl.BlockSpec((lat_count, features), at)),
            (mod, vector(1, 3 * features)),
            (grad_tok, row(group_len, features)),
            (grad_lat, row(lat_count, features)),
            (grad_att, row(length, features)),
            (triple_all, row(length, 6 * half)),
            (stats_all, vector(2 * heads, length)),
        ]
        + [(piece, ANY) for piece in own_w + other_w],
        [
            ((mine * group_len, features), UPPER, row(group_len, features)),
            ((mine * lat_count, features), UPPER, row(lat_count, features)),
            ((mine * length, features), LOWER, row(length, features)),
            ((mine * length, 6 * half), LOWER, row(length, 6 * half)),
            ((mine, 2, features), UPPER, vector(2, features)),
            (tokens.shape, UPPER, pl.BlockSpec((group_len, features), at)),
        ],
        [
            pltpu.VMEM((features, 6 * half), LOWER),
            pltpu.VMEM((features, 2 * half), LOWER),
            pltpu.SemaphoreType.DMA((4 * np_ * own_w[0].shape[0],)),
        ],
        grid=(count,),
        flops=count * length * features * features * 20,
        moved=count * 5_000_000,
        name="attention_backward",
        aliased=before,
        after=after,
    )


def attention_gradients(move, side, inputs, triples, grad_att, mixed, half, came=(), after=()):
    total, features = inputs.shape
    nb, nk = move.blocks
    columns = 4 * half

    def kernel(info, in_ref, tri_ref, att_ref, mix_ref, *refs):
        first = mm(jnp.transpose(in_ref[...]), tri_ref[...])
        second = mm(jnp.transpose(att_ref[...]), mix_ref[...])
        if side == 1:
            refs[0][:, : 3 * half] = first.astype(LOWER)
            refs[0][:, 3 * half :] = second.astype(LOWER)
        else:
            other, grads, square = refs[0], refs[1:-1], refs[-1]
            square[:, : 3 * half] = (first + other[:, : 3 * half].astype(UPPER)).astype(LOWER)
            square[:, 3 * half :] = (second + other[:, 3 * half :].astype(UPPER)).astype(LOWER)
            place(info, move.goes_at, square, grads, 0, columns)

    rows = [features // nb] * nb if side == 0 else [features]
    return call(
        kernel,
        move.info,
        [
            (inputs, whole(inputs.shape)),
            (triples, pl.BlockSpec((total, 3 * half), lambda i, info: (0, side))),
            (grad_att, whole(grad_att.shape)),
            (mixed, pl.BlockSpec((total, half), lambda i, info: (0, side))),
        ]
        + [(part, whole(part.shape)) for part in came],
        [((size, columns), LOWER, whole((size, columns))) for size in rows],
        [pltpu.VMEM((features, columns), LOWER)] if side == 0 else [],
        flops=total * features * columns * 2,
        moved=total * (features + columns) * 2,
        name="attention_gradients",
        after=after,
    )


ROOT = 0.7978845608028654
CUBE = 0.044715


def feed_forward(rows, grad_result, shift, scale, gate, w_up, w_down, hidden_ref, upward_ref, step=768):
    normed, inverse = normalize(rows)
    inputs = (normed * (1.0 + scale) + shift).astype(LOWER)
    grad_narrow = (gate * grad_result).astype(LOWER)
    narrowed = grad_inputs = 0.0
    for start in range(0, w_up.shape[1], step):
        units = slice(start, start + step)
        upward = mm(inputs, w_up[:, units])
        square = upward * upward
        bend = jnp.tanh(upward * (ROOT + (ROOT * CUBE) * square))
        half_up = 0.5 * upward
        hidden = (half_up * (1.0 + bend)).astype(LOWER)
        slope = 0.5 * (1.0 + bend) + half_up * (1.0 - bend * bend) * (
            ROOT + (3.0 * ROOT * CUBE) * square
        )
        grad_upward = (mm(grad_narrow, w_down[:, units]) * slope).astype(LOWER)
        hidden_ref[:, units] = hidden
        upward_ref[:, units] = grad_upward
        narrowed = narrowed + mm_nt(hidden, w_down[:, units])
        grad_inputs = grad_inputs + mm_nt(grad_upward, w_up[:, units])
    result = rows + gate * narrowed
    grad_rows = grad_result + norm_back(grad_inputs * (1.0 + scale), normed, inverse)
    return result, grad_rows, inputs, grad_narrow, (
        grad_inputs,
        grad_inputs * normed,
        grad_result * narrowed,
    )


def bring_wide(wide, w_up, w_down, sems):
    units = w_up.shape[1] // 2
    count, rows, _ = wide.shape
    copies = []
    for entry in range(count):
        at = pl.ds(entry // 2 * rows, rows)
        for which, target in enumerate((w_up, w_down)):
            copies.append(
                pltpu.make_async_copy(
                    wide.at[entry, :, pl.ds(which * units, units)],
                    target.at[at, pl.ds(entry % 2 * units, units)],
                    sems.at[2 * entry + which],
                )
            )
    for copy in copies:
        copy.start()
    for copy in copies:
        copy.wait()


def token_feed_forward(move, first, count, rows, cotangent, mod, wide_w, sizes, before=(), after=()):
    group_len, lat_count, features, half = sizes
    groups = cotangent.shape[0] // group_len
    units = wide_w.shape[2] // 2

    def kernel(info, row_ref, cot, mod_ref, *refs):
        wide = refs[0]
        result, grad, inputs_ref, narrow_ref, hidden_ref, upward_ref, vec, full = refs[1:9]
        w_up, w_down, sems = refs[9:]

        @pl.when(pl.program_id(0) == 0)
        def _():
            bring_wide(wide, w_up, w_down, sems)

        shift, scale, gate = [mod_ref[0, :, i * features : (i + 1) * features] for i in range(3)]
        out, grad_rows, inputs, narrow, terms = feed_forward(
            row_ref[...], cot[...], shift, scale, gate, w_up, w_down, hidden_ref, upward_ref
        )
        result[...] = out
        full[...] = out
        grad[...] = grad_rows
        inputs_ref[...] = jnp.transpose(inputs)
        narrow_ref[...] = jnp.transpose(narrow)
        for number, term in enumerate(terms):
            vec[0, number : number + 1, :] = jnp.sum(term, 0, keepdims=True)

    at = pl.BlockSpec((group_len, features), lambda g, info: (info[0] * groups // 2 + first + g, 0))
    turned = pl.BlockSpec((features, group_len), lambda g, info: (0, first + g))
    row = lambda columns: pl.BlockSpec((group_len, columns), lambda g, info: (first + g, 0))
    total = rows.shape[0]
    return call(
        kernel,
        move.info,
        [
            (rows, row(features)),
            (
                cotangent,
                at,
            ),
            (mod, pl.BlockSpec((1, 1, 3 * features), lambda g, info: (first + g, 0, 0))),
        ]
        + [(wide_w, ANY)],
        [
            ((total, features), UPPER, row(features)),
            ((total, features), UPPER, row(features)),
            ((features, total), LOWER, turned),
            ((features, total), LOWER, turned),
            ((total, 2 * units), LOWER, row(2 * units)),
            ((total, 2 * units), LOWER, row(2 * units)),
            ((groups // 2, 3, features), UPPER, pl.BlockSpec((1, 3, features), lambda g, info: (first + g, 0, 0))),
            (cotangent.shape, UPPER, at),
        ],
        [
            pltpu.VMEM((features, 2 * units), LOWER),
            pltpu.VMEM((features, 2 * units), LOWER),
            pltpu.SemaphoreType.DMA((2 * wide_w.shape[0],)),
        ],
        grid=(count,),
        flops=count * group_len * features * units * 16,
        moved=count * 8_000_000,
        name="token_feed_forward",
        aliased=before,
        after=after,
    )


def latent_feed_forward(move, lat_one, branch, came, cotangent, mod, wide_w, sizes, after=()):
    group_len, lat_count, features, half = sizes
    rows_n = lat_one.shape[0]
    count = rows_n // lat_count
    units = wide_w.shape[2] // 2

    def kernel(info, one, own, other, cot, mod_ref, *refs):
        wide = refs[0]
        result, grad, inputs_ref, narrow_ref, hidden_ref, upward_ref, vec = refs[1:8]
        w_up, w_down, sems = refs[8:]
        bring_wide(wide, w_up, w_down, sems)
        vectors = [
            jnp.concatenate(
                [
                    jnp.broadcast_to(mod_ref[g, :, i * features : (i + 1) * features], (lat_count, features))
                    for g in range(count)
                ],
                0,
            )
            for i in range(3)
        ]
        rows = one[...] + own[...] + other[...]
        out, grad_rows, inputs, narrow, terms = feed_forward(
            rows, cot[...], *vectors, w_up, w_down, hidden_ref, upward_ref
        )
        result[...] = out
        grad[...] = grad_rows
        inputs_ref[...] = inputs
        narrow_ref[...] = narrow
        for number, term in enumerate(terms):
            for g in range(count):
                vec[g, number : number + 1, :] = jnp.sum(
                    term[g * lat_count : (g + 1) * lat_count], 0, keepdims=True
                )

    rows_f = (rows_n, features)
    return call(
        kernel,
        move.info,
        [
            (lat_one, whole(rows_f)),
            (branch, whole(rows_f)),
            (came, whole(rows_f)),
            (cotangent, pl.BlockSpec(rows_f, lambda i, info: (info[0], 0))),
            (mod, whole(mod.shape)),
        ]
        + [(wide_w, ANY)],
        [
            (rows_f, UPPER, whole(rows_f)),
            (rows_f, UPPER, whole(rows_f)),
            (rows_f, LOWER, whole(rows_f)),
            (rows_f, LOWER, whole(rows_f)),
            ((rows_n, 2 * units), LOWER, whole((rows_n, 2 * units))),
            ((rows_n, 2 * units), LOWER, whole((rows_n, 2 * units))),
            ((count, 3, features), UPPER, whole((count, 3, features))),
        ],
        [
            pltpu.VMEM((features, 2 * units), LOWER),
            pltpu.VMEM((features, 2 * units), LOWER),
            pltpu.SemaphoreType.DMA((2 * wide_w.shape[0],)),
        ],
        flops=rows_n * features * units * 64,
        moved=12_000_000,
        name="latent_feed_forward",
        after=after,
    )


def wide_gradients(move, side, lefts, rights, lat_lefts, lat_rights, came=(), before=(), after=(), tile=768):
    features, total = lefts[0].shape
    units = rights[0].shape[1] // 2
    tiles = units // tile
    nb, nk = move.blocks
    extra = len(came)

    def kernel(info, *refs):
        outs = refs[8 + extra :]
        step = pl.program_id(1)
        for which in range(2):
            left, right, lat_left, lat_right = [refs[2 * number + which] for number in range(4)]

            @pl.when(pl.program_id(0) == which)
            def _():
                acc = mm_tn(lat_left[...], lat_right[...]) + mm(left[...], right[...])
                if side == 1:
                    outs[0][...] = acc.astype(LOWER)
                else:
                    outs[-1][...] = (acc + refs[8][...].astype(UPPER)).astype(LOWER)

        if side == 0:
            place_square(move.staged, outs[-1], outs[0], 0, tile)

    def columns(rows, which):
        def at(w, s, info):
            core = info[0] if side == 0 else 1 - info[0]
            held = (tiles - 1) if which == 0 else 0
            return (0, core * tiles + jnp.where(w == which, s, held))

        return pl.BlockSpec((rows, tile), at)

    here = lambda w, s, info: (0, w * tiles + s)
    offset = 0 if side == 1 else before[0].shape[1] // tile - 2 * tiles
    out_at = lambda w, s, info: (0, offset + w * tiles + s)
    shapes = [part.shape for part in before] if side == 0 else [(features, 2 * units)]
    return call(
        kernel,
        move.info,
        [(part, whole(part.shape)) for part in lefts]
        + [(part, columns(part.shape[0], which)) for which, part in enumerate(rights)]
        + [(part, whole(part.shape)) for part in lat_lefts]
        + [(part, columns(part.shape[0], which)) for which, part in enumerate(lat_rights)]
        + [(part, pl.BlockSpec((features, tile), here)) for part in came],
        [(shape, LOWER, pl.BlockSpec((shape[0], tile), out_at)) for shape in shapes],
        [pltpu.VMEM((features, tile), LOWER)] if side == 0 else [],
        grid=(2, tiles),
        flops=total * features * units * 4,
        moved=total * units * 4 + features * units * 4,
        name="wide_gradients",
        aliased=before,
        after=after,
    )


def modulation_terms(move, vectors, modulator, bias, middle):
    shard, width = modulator.shape
    size = middle // 2
    nb = len(vectors)
    count = vectors[0].shape[0]
    rows = vectors[0].shape[1]
    chips = count * rows // SLOT
    features = vectors[0].shape[2]

    def kernel(info, *refs):
        pieces = refs[:nb]
        mods, biases = refs[nb : nb + 2], refs[nb + 2 : nb + 4]
        outs = refs[nb + 4 :]
        terms, picked, gain = outs[:nb], outs[nb : 2 * nb], outs[2 * nb]
        shape = (features, shard)
        select = lax.broadcasted_iota(jnp.int32, shape, 0) == (
            lax.broadcasted_iota(jnp.int32, shape, 1) + info[1] * shard
        )
        select = jnp.where(select, 1.0, 0.0).astype(LOWER)
        gains = jnp.zeros((1, features), UPPER)
        for b in range(nb):
            value = pieces[b][...].reshape(chips * SLOT, features)
            gains = gains + jnp.sum(
                value.astype(UPPER).reshape(chips, SLOT, features)[:, 8:9, :], 0
            )
            mine = mm(value, select)
            picked[b][...] = jnp.concatenate(
                [
                    jnp.where(
                        info[0] == 0,
                        mine[k * SLOT : k * SLOT + 4],
                        mine[k * SLOT + 4 : k * SLOT + 8],
                    )
                    for k in range(chips)
                ],
                0,
            )
            for part in range(2):
                product = mm(mine.astype(LOWER), mods[part][...].astype(LOWER)) + biases[part][...]
                product = product.reshape(chips, SLOT, size)
                for k in range(chips):
                    where = (chips - k) % chips if nb > 1 else k
                    terms[b][where, :, part * size : (part + 1) * size] = product[k, :8]
        gain[...] = gains

    columns = lambda rows_, part: pl.BlockSpec((rows_, size), lambda i, info: (0, 2 * part + info[0]))
    return call(
        kernel,
        move.info,
        [(piece, whole(piece.shape)) for piece in vectors]
        + [(modulator, columns(shard, 0)), (modulator, columns(shard, 1))]
        + [(bias, columns(1, 0)), (bias, columns(1, 1))],
        [((chips, 8, 2 * size), UPPER, whole((chips, 8, 2 * size)))] * nb
        + [((chips * 4, shard), UPPER, whole((chips * 4, shard)))] * nb
        + [((1, features), UPPER, whole((1, features)))],
        flops=10_000_000,
        moved=3_000_000,
        name="modulation_terms",
    )


def modulation_gradients(move, picked, grads, modulator, dp_size, after=()):
    shard, width = modulator.shape
    features = width // 6
    nb = len(grads)
    chips = dp_size // nb
    own = 4

    def kernel(info, *refs):
        picks, parts = refs[:nb], refs[nb : 2 * nb]
        mod_ref, out, terms = refs[2 * nb :]
        products = [jnp.zeros((chips * own, shard), UPPER) for _ in range(nb)]
        for i in range(6):
            at = slice(i * features, (i + 1) * features)
            weight = mod_ref[:, at].astype(LOWER)
            total = jnp.zeros((shard, features), UPPER)
            sums = jnp.zeros((1, features), UPPER)
            for b in range(nb):
                value = parts[b][:, i // 2 * 8 : i // 2 * 8 + 8, :].astype(UPPER)
                value = jnp.concatenate(
                    [value[k, i % 2 * own : (i % 2 + 1) * own] for k in range(chips)], 0
                )
                sums = sums + jnp.sum(value, 0, keepdims=True)
                value = value.astype(LOWER)
                total = total + mm_tn(picks[b][...].astype(LOWER), value)
                products[b] = products[b] + mm_nt(value, weight)
            out[:shard, at] = total
            extra = jnp.zeros((1, features), UPPER)
            if i == 0:
                for b in range(nb):
                    for k in range(chips):
                        extra = extra + jnp.sum(parts[b][k, 24:32, :].astype(UPPER), 0, keepdims=True)
            out[shard:, at] = jnp.concatenate(
                [sums, extra, jnp.zeros((6, features), UPPER)], 0
            )
        for b in range(nb):
            for k in range(chips):
                terms[info[move.chips_at + b * chips + k]] = products[b][k * own : (k + 1) * own]

    return call(
        kernel,
        move.info,
        [(piece, whole(piece.shape)) for piece in picked]
        + [(piece, whole(piece.shape)) for piece in grads]
        + [(modulator, whole(modulator.shape))],
        [
            ((shard + 8, width), UPPER, whole((shard + 8, width))),
            ((dp_size, own, shard), UPPER, whole((dp_size, own, shard))),
        ],
        flops=10_000_000,
        moved=3_000_000,
        name="modulation_gradients",
        after=after,
    )


def latent_project(move, own, other, gain, weights, half):
    rows_n, features = own.shape
    np_ = len(weights)

    def kernel(info, own_ref, other_ref, gain_ref, *refs):
        pieces = refs[:np_]
        triple, lat_in, weight, rows, sems = refs[np_:]
        copies = bring(info, move.came_at, pieces, [(weight, 0, 0, 4 * half)], sems)
        here = pl.multiple_of(info[0] * rows_n, rows_n)
        there = pl.multiple_of((1 - info[0]) * rows_n, rows_n)
        rows[pl.ds(here, rows_n), :] = own_ref[...]
        rows[pl.ds(there, rows_n), :] = other_ref[...]
        normed, _ = normalize(rows[...])
        inputs = (normed * gain_ref[...]).astype(LOWER)
        lat_in[...] = inputs
        for copy in copies:
            copy.wait()
        triple[...] = mm(inputs, weight[:, : 3 * half]).astype(LOWER)

    total = 2 * rows_n
    shapes = [(total, 3 * half), (total, features), (features, 4 * half)]
    return call(
        kernel,
        move.info,
        [(own, whole(own.shape)), (other, whole(own.shape)), (gain, whole(gain.shape))]
        + [(piece, ANY) for piece in weights],
        [(shape, LOWER, whole(shape)) for shape in shapes],
        [
            pltpu.VMEM((total, features), UPPER),
            pltpu.SemaphoreType.DMA((np_ * weights[0].shape[0],)),
        ],
        flops=500_000_000,
        moved=6_000_000,
        name="latent_project",
    )


def allowed_pairs(info, own_image, image, keep, own_keep=None):
    count, total = own_image.shape[0], image.shape[1]
    shape = (count, total)
    itself = lax.broadcasted_iota(jnp.int32, shape, 1) == (
        lax.broadcasted_iota(jnp.int32, shape, 0) + info[1] * count
    )
    kept = (keep if own_keep is None else own_keep) == 1
    return (own_image == image) & (kept | itself)


def split_rows(info, full, own, other):
    rows = own.shape[0]
    own[...] = full[pl.ds(pl.multiple_of(info[0] * rows, rows), rows), :]
    other[...] = full[pl.ds(pl.multiple_of((1 - info[0]) * rows, rows), rows), :]


def latent_forward(move, query, key_values, weights, masks, half, features, after=()):
    count = query.shape[0]
    np_ = len(key_values)
    total = np_ * key_values[0].shape[0] * count
    heads = half // HD

    def kernel(info, query_ref, weight, own_image, image, keep, *refs):
        pieces = refs[:np_]
        mixed, stats, own, other, all_kv, full, sems = refs[np_:]
        copies = bring(info, move.chips_at, pieces, [(all_kv, 0, half, 2 * half)], sems)
        allowed = allowed_pairs(info, own_image[...], image[...], keep[...])
        for copy in copies:
            copy.wait()
        lane = lax.broadcasted_iota(jnp.int32, (count, 128), 1)
        logs = jnp.zeros((count, 128), UPPER)
        outs = []
        for head in range(heads):
            at = slice(head * HD, (head + 1) * HD)
            scores = mm_nt(query_ref[:, at], all_kv[:, at]) * SCALING
            scores = jnp.where(allowed, scores, NEVER)
            peak = jnp.max(scores, 1, keepdims=True)
            weights_ = jnp.exp(scores - peak)
            sums = jnp.sum(weights_, 1, keepdims=True)
            logs = jnp.where(lane == head, peak + jnp.log(sums), logs)
            weights_ = (weights_ * (1.0 / sums)).astype(LOWER)
            outs.append(mm(weights_, all_kv[:, half + head * HD : half + (head + 1) * HD]).astype(LOWER))
        stats[...] = logs
        mixed[...] = jnp.concatenate(outs, 1)
        full[...] = mm_nt(mixed[...], weight[:, 3 * half :])
        split_rows(info, full, own, other)

    part = (count // 2, features)
    return call(
        kernel,
        move.info,
        [(query, whole(query.shape)), (weights, whole(weights.shape))]
        + [(mask, whole(mask.shape)) for mask in masks[:3]]
        + [(piece, ANY) for piece in key_values],
        [
            ((count, half), LOWER, whole((count, half))),
            ((count, 128), UPPER, whole((count, 128))),
            (part, UPPER, whole(part)),
            (part, UPPER, whole(part)),
        ],
        [
            pltpu.VMEM((total, 2 * half), LOWER),
            pltpu.VMEM((count, features), UPPER),
            pltpu.SemaphoreType.DMA((np_ * key_values[0].shape[0],)),
        ],
        flops=1_000_000_000,
        moved=6_000_000,
        name="latent_forward",
        after=after,
    )


def latent_backward(move, query, key_values, weights, masks, mixed, stats, grad_own, grad_other, half, features):
    count = query.shape[0]
    np_ = len(key_values)
    total = np_ * key_values[0].shape[0] * count
    heads = half // HD

    def kernel(info, query_ref, weight, own_image, image, keep, mixed_ref, stats_ref, own, other, *refs):
        pieces = refs[:np_]
        sent, grad_query, out_grad, all_kv, full, sems = refs[np_:]
        copies = bring(info, move.chips_at, pieces, [(all_kv, 0, half, 2 * half)], sems)
        allowed = allowed_pairs(info, own_image[...], image[...], keep[...])
        rows_n = own.shape[0]
        full[pl.ds(pl.multiple_of(info[0] * rows_n, rows_n), rows_n), :] = own[...]
        full[pl.ds(pl.multiple_of((1 - info[0]) * rows_n, rows_n), rows_n), :] = other[...]
        branch = full[...].astype(LOWER)
        grad_mixed = mm(branch, weight[:, 3 * half :]).astype(LOWER)
        out_grad[...] = mm_tn(branch, mixed_ref[...])
        sent[:, :half] = grad_mixed
        for copy in copies:
            copy.wait()
        lane = lax.broadcasted_iota(jnp.int32, (count, 128), 1)
        extra = jnp.zeros((count, 128), UPPER)
        outs = []
        for head in range(heads):
            at = slice(head * HD, (head + 1) * HD)
            scores = mm_nt(query_ref[:, at], all_kv[:, at]) * SCALING
            log_total = stats_ref[:, head : head + 1]
            weights_ = jnp.exp(jnp.where(allowed, scores - log_total, NEVER))
            grad_weights = mm_nt(grad_mixed[:, at], all_kv[:, half + head * HD : half + (head + 1) * HD])
            delta = jnp.sum(grad_weights * weights_, 1, keepdims=True)
            grad_scores = (weights_ * (grad_weights - delta)).astype(LOWER)
            outs.append((mm(grad_scores, all_kv[:, at]) * SCALING).astype(LOWER))
            for start, column in ((0, log_total), (3, delta)):
                high = column.astype(LOWER).astype(UPPER)
                middle = (column - high).astype(LOWER).astype(UPPER)
                low = column - high - middle
                for number, part in enumerate((high, middle, low)):
                    extra = jnp.where(lane == (start + number) * heads + head, part, extra)
        sent[:, half:] = extra.astype(LOWER)
        grad_query[...] = jnp.concatenate(outs, 1)

    return call(
        kernel,
        move.info,
        [(query, whole(query.shape)), (weights, whole(weights.shape))]
        + [(mask, whole(mask.shape)) for mask in masks[:3]]
        + [(value, whole(value.shape)) for value in (mixed, stats, grad_own, grad_other)]
        + [(piece, ANY) for piece in key_values],
        [
            ((count, half + 128), LOWER, whole((count, half + 128))),
            ((count, half), LOWER, whole((count, half))),
            ((features, half), UPPER, whole((features, half))),
        ],
        [
            pltpu.VMEM((total, 2 * half), LOWER),
            pltpu.VMEM((count, features), UPPER),
            pltpu.SemaphoreType.DMA((np_ * key_values[0].shape[0],)),
        ],
        flops=1_500_000_000,
        moved=6_000_000,
        name="latent_backward",
    )


def latent_sources(move, key_value, gathered, came, weights, masks, grad_query, lat_in, out_grad, lat_own, lat_other, gain, half, features, room, after=()):
    count = key_value.shape[0]
    np_ = len(came)
    total = np_ * came[0].shape[0] * count
    heads = half // HD
    nb, nk = move.blocks

    def kernel(info, kv, weight, own_image, image, own_keep, grad_query_ref, lat_in_ref, out_grad_ref, lat_o, lat_t, gain_ref, *refs):
        pieces, gathered_refs = refs[:np_], refs[np_ : 2 * np_]
        refs = refs[np_:]
        own, other, gain_rows = refs[np_ : np_ + 3]
        grads = refs[np_ + 3 : np_ + 4]
        all_q, full, rows, square, sems = refs[np_ + 4 :]
        number = sems.shape[0] // 2
        copies = bring(
            info, move.chips_at, pieces, [(all_q, half, 0, half + 128)], sems.at[pl.ds(0, number)]
        ) + bring(
            info, move.chips_at, gathered_refs, [(all_q, 0, 0, half)], sems.at[pl.ds(number, number)]
        )
        allowed = allowed_pairs(info, own_image[...], image[...], None, own_keep[...])
        for copy in copies:
            copy.wait()
        turned = jnp.transpose(all_q[:, 2 * half :].astype(UPPER))
        keys, values = [], []
        for head in range(heads):
            at = slice(head * HD, (head + 1) * HD)
            other_at = slice(half + head * HD, half + (head + 1) * HD)
            last_at = slice(2 * half + head * HD, 2 * half + (head + 1) * HD)
            log_total, delta = [
                sum(turned[(s + i) * heads + head : (s + i) * heads + head + 1] for i in range(3))
                for s in (0, 3)
            ]
            scores = mm_nt(kv[:, other_at], all_q[:, at]) * SCALING
            weights_ = jnp.exp(jnp.where(allowed, scores - log_total, NEVER))
            grad_weights = mm_nt(kv[:, last_at], all_q[:, other_at])
            grad_scores = (weights_ * (grad_weights - delta)).astype(LOWER)
            keys.append((mm(grad_scores, all_q[:, at]) * SCALING).astype(LOWER))
            values.append(mm(weights_.astype(LOWER), all_q[:, other_at]).astype(LOWER))
        triple = jnp.concatenate([grad_query_ref[...]] + keys + values, 1)
        full[...] = mm_nt(triple, weight[:, : 3 * half])
        split_rows(info, full, own, other)
        rows_n = lat_o.shape[0]
        rows[pl.ds(pl.multiple_of(info[0] * rows_n, rows_n), rows_n), :] = lat_o[...]
        rows[pl.ds(pl.multiple_of((1 - info[0]) * rows_n, rows_n), rows_n), :] = lat_t[...]
        normed, _ = normalize(rows[...])
        square[:, : 3 * half] = mm_tn(lat_in_ref[...], triple).astype(LOWER)
        square[:, 3 * half : 4 * half] = out_grad_ref[...].astype(LOWER)
        total_gain = jnp.sum(full[...] * normed, 0, keepdims=True)
        for number in range(3):
            part = total_gain.astype(LOWER).astype(UPPER)
            gain_rows[number : number + 1, :] = part
            total_gain = total_gain - part
        gain_rows[3:, :] = jnp.zeros((5, features), UPPER)
        place_square(move.staged, square, grads[0], 0, 4 * half)

    part = (count // 2, features)
    columns = 4 * half
    return call(
        kernel,
        move.info,
        [(key_value, whole(key_value.shape)), (weights, whole(weights.shape))]
        + [(mask, whole(mask.shape)) for mask in (masks[0], masks[1], masks[3])]
        + [
            (value, whole(value.shape))
            for value in (grad_query, lat_in, out_grad, lat_own, lat_other, gain)
        ]
        + [(piece, ANY) for piece in came + gathered],
        [(part, UPPER, whole(part))] * 2
        + [((8, features), UPPER, whole((8, features)))]
        + [((features, columns + room), LOWER, whole((features, columns)))],
        [
            pltpu.VMEM((total, 2 * half + 128), LOWER),
            pltpu.VMEM((count, features), UPPER),
            pltpu.VMEM((count, features), UPPER),
            pltpu.VMEM((features, columns), LOWER),
            pltpu.SemaphoreType.DMA((2 * np_ * came[0].shape[0],)),
        ],
        flops=2_000_000_000,
        moved=8_000_000,
        name="latent_sources",
        after=after,
    )


def fill(move, full, other, after=(), block=512):
    rows, features = other.shape
    block = min(block, rows)
    steps = rows // block

    def kernel(info, other_ref, out):
        out[...] = other_ref[...]

    return call(
        kernel,
        move.info,
        [(other, pl.BlockSpec((block, features), lambda i, info: (i, 0)))],
        [
            (
                full.shape,
                UPPER,
                pl.BlockSpec((block, features), lambda i, info: ((1 - info[0]) * steps + i, 0)),
            )
        ],
        grid=(steps,),
        moved=2 * rows * features * 4,
        name="fill",
        after=after,
        aliased=[full],
    )[0]


def make_body(dp_size):
    def body(
        tokens,
        latents,
        condition,
        modulator,
        offsets,
        local_qkv,
        local_out,
        global_qkv,
        global_out,
        latent_gain,
        up_weight,
        down_weight,
        group_image,
        latent_keep,
        token_cotangent,
        latent_cotangent,
    ):
        move = Moves(dp_size)
        mp, dp = move.mp, move.dp
        groups = condition.shape[0]
        own = groups // 2
        features = tokens.shape[1]
        group_len = tokens.shape[0] // groups
        lat_count = latents.shape[0] // groups
        shard, width = modulator.shape
        half = local_out.shape[1]
        units = up_weight.shape[1]
        middle = width // 2
        sizes = (group_len, lat_count, features, half)

        def mine(value):
            size = value.shape[0] // 2
            return lax.dynamic_slice_in_dim(value, mp * size, size, 0)

        def others(value):
            size = value.shape[0] // 2
            return lax.dynamic_slice_in_dim(value, (1 - mp) * size, size, 0)

        scaled = jax.nn.silu(condition).astype(LOWER)
        gain_row = lax.dynamic_update_slice(
            jnp.zeros((1, features), LOWER), latent_gain.astype(LOWER)[None], (0, dp * shard)
        )
        bias_row = lax.dynamic_update_slice(
            jnp.zeros((1, width), UPPER),
            offsets.astype(LOWER).astype(UPPER)[None],
            (0, dp * (width // dp_size)),
        )
        vectors = move.spread(
            move.line(
                jnp.concatenate(
                    [scaled, gain_row, jnp.zeros((SLOT - 1 - groups, features), LOWER)], 0
                )
            )
        )
        found = modulation_terms(move, vectors, modulator, bias_row, middle)
        nb = len(vectors)
        picked, gain = found[nb : 2 * nb], found[2 * nb]

        total = move.finish(
            move.fold(move.meet([term.reshape(-1, term.shape[2]) for term in found[:nb]]))
        )
        total, came = mine(total), move.swap(others(total))
        mod_one, mod_two = [
            move.in_order(total[:, part], came[:, part], 1)[:, None]
            for part in (slice(0, middle // 2), slice(middle // 2, middle))
        ]

        wide_shard = jnp.concatenate([up_weight, down_weight], 1).astype(LOWER)
        if move.staged:
            wide_w = lax.all_gather(wide_shard, ("dp", "mp"), axis=0)
        else:
            wide_w = lax.all_gather(
                lax.all_gather(wide_shard, "dp", axis=0, tiled=True), "mp", axis=0
            )
        shards = jnp.concatenate(
            [
                local_qkv.reshape(shard, 3 * half),
                local_out,
                global_qkv.reshape(shard, 3 * half),
                global_out,
            ],
            1,
        ).astype(LOWER)
        if move.staged:
            turned = [shards] + [move.turn(shards, step) for step in (1, 2, 3)]
            first_line, lat_line = [
                jnp.stack([part[:, start : start + 4 * half] for part in turned])
                for start in (0, 4 * half)
            ]
        else:
            first_line, lat_line = shards[:, : 4 * half], shards[:, 4 * half :]
        first_w = move.spread(first_line)
        first_other = [move.swap(piece) for piece in first_w]
        latent_w = move.spread(wait_for(lat_line, first_w[-1]))

        after, lat_one, triple, stats, mixed, attended = attention_forward(
            move, 0, own, tokens, latents, mod_one, first_w, first_other, sizes
        )


        chip_count = groups * lat_count
        images = jnp.repeat(group_image, lat_count)
        own_slice = lambda value: lax.dynamic_slice_in_dim(value, dp * chip_count, chip_count)
        masks = (
            own_slice(images)[:, None],
            images[None],
            latent_keep[None],
            own_slice(latent_keep)[:, None],
        )
        lat_came = move.swap(lat_one)
        lat_triple, lat_in, lat_weight = latent_project(
            move, lat_one, lat_came, gain, latent_w, half
        )
        key_values_line = move.line(lat_triple)
        key_values = move.spread(key_values_line, chips=True)

        part = own // 2
        ff = token_feed_forward(
            move, 0, part, after, token_cotangent, mod_two, wide_w, sizes, after=[key_values_line]
        )
        lat_mixed, lat_stats, branch_own, branch_other = latent_forward(
            move, lat_triple, key_values, lat_weight, masks, half, features, after=[ff[6]]
        )
        lat_result, grad_lat_two, lat_inputs, lat_narrow, lat_hidden, lat_upward, lat_vec = (
            latent_feed_forward(
                move,
                lat_one,
                branch_own,
                move.swap(branch_other),
                latent_cotangent,
                mod_two,
                wide_w,
                sizes,
            )
        )

        sent, grad_query, out_grad = latent_backward(
            move,
            lat_triple,
            key_values,
            lat_weight,
            masks,
            lat_mixed,
            lat_stats,
            grad_lat_two,
            move.swap(grad_lat_two),
            half,
            features,
        )
        came_line = move.line(sent)
        came = move.spread(came_line, chips=True)
        ff = token_feed_forward(
            move, part, own - part, after, token_cotangent, mod_two, wide_w, sizes, ff, [sent]
        )
        token_result, grad_tok, ff_inputs, ff_narrow, ff_hidden, ff_upward, ff_vec, token_output = ff
        factors = (
            [ff_inputs, ff_narrow],
            [ff_upward, ff_hidden],
            [lat_inputs, lat_narrow],
            [lat_upward, lat_hidden],
        )
        (wide_other,) = wide_gradients(move, 1, *factors, after=[came_line])
        lat_grad_own, lat_grad_other, gain_rows, *lat_parts = latent_sources(
            move,
            lat_triple,
            key_values,
            came,
            lat_weight,
            masks,
            grad_query,
            lat_in,
            out_grad,
            lat_one,
            lat_came,
            gain,
            half,
            features,
            2 * units,
            after=[wide_other],
        )
        (early_parts,) = wide_gradients(
            move, 0, *factors, came=[move.swap(wide_other)], before=lat_parts
        )
        early_line = move.square_to_line(early_parts)
        grad_lat_one, grad_att, gate_vec = attention_entry(
            move,
            lat_grad_own,
            move.swap(lat_grad_other),
            lat_one,
            grad_lat_two,
            gain,
            mod_one,
            grad_tok,
            attended,
            sizes,
            after=[early_parts],
        )

        token_output = fill(move, token_output, move.swap(token_result), [wide_other])

        grad_tokens, grad_latents, first_in, first_triples, vec_one, grad_output = attention_backward(
            move,
            0,
            own,
            tokens,
            latents,
            mod_one,
            grad_tok,
            grad_lat_one,
            grad_att,
            (triple, stats),
            first_w,
            first_other,
            sizes,
            after=[token_output],
        )
        vec_two = ff_vec + lat_vec
        vectors = jnp.concatenate(
            [vec_one[:, 0], vec_one[:, 1], gate_vec[:, 0]]
            + [vec_two[:, i] for i in range(3)]
            + [gain_rows],
            0,
        ).astype(LOWER)
        vectors_line = move.line(vectors)
        first_factors = (first_in, first_triples, grad_att, mixed, half)
        (first_grads_other,) = attention_gradients(move, 1, *first_factors, after=[vectors])
        first_parts = attention_gradients(
            move, 0, *first_factors, [move.swap(first_grads_other)], [vectors_line]
        )
        first_terms = move.meet(first_parts)
        early_sum = move.line_to_own(early_line)
        mod_grad, grad_terms = modulation_gradients(
            move,
            picked,
            move.spread(vectors_line, chips=True),
            modulator,
            dp_size,
            after=[first_parts[0], early_line],
        )
        grad_output = fill(move, grad_output, move.swap(grad_tokens))
        first_sum = move.finish(
            move.fold(wait_for(first_terms, grad_output, mod_grad))
        )
        mod_grad = mod_grad + move.swap(mod_grad)
        grad_scaled = lax.all_to_all(grad_terms, "dp", 0, 0, tiled=True)
        grad_scaled = grad_scaled.transpose(1, 0, 2).reshape(own, features)
        grad_scaled = move.in_order(grad_scaled, move.swap(grad_scaled))
        grad_condition = jax.vjp(jax.nn.silu, condition)[1](grad_scaled)[0]
        bias_all = mod_grad[shard]
        gain_grad = lax.dynamic_slice_in_dim(mod_grad[shard + 1, :features], dp * shard, shard)
        piece = width // dp_size
        latent_output = move.in_order(lat_result, move.swap(lat_result))
        return (
            token_output,
            latent_output,
            grad_output,
            move.in_order(grad_latents, move.swap(grad_latents)),
            grad_condition,
            mod_grad[:shard],
            lax.dynamic_slice_in_dim(bias_all, dp * piece, piece),
            first_sum[:, : 3 * half].reshape(shard, 3, half),
            first_sum[:, 3 * half :],
            early_sum[:, : 3 * half].reshape(shard, 3, half),
            early_sum[:, 3 * half : 4 * half],
            gain_grad,
            early_sum[:, 4 * half : 4 * half + units],
            early_sum[:, 4 * half + units :],
        )

    return body


def solution(mesh):
    rows, heads = P("dp", None), P("dp", None, "mp")
    columns, vector = P("dp", "mp"), P("dp")
    return jax.shard_map(
        make_body(mesh.shape["dp"]),
        mesh=mesh,
        in_specs=(
            rows, rows, rows, rows, vector, heads, columns, heads, columns, vector,
            columns, columns, P(), P(), rows, rows,
        ),
        out_specs=(
            rows, rows, rows, rows, rows, rows, vector, heads, columns, heads, columns,
            vector, columns, columns,
        ),
        check_vma=False,
    )
```

```python
import jax
import jax.numpy as jnp
from jax import lax
from jax.experimental import pallas as pl
from jax.experimental.pallas import tpu as pltpu
from jax.sharding import PartitionSpec as P

HD = 64
EPSILON = 1e-06
SCALING = HD**-0.5
LOWER = jnp.bfloat16
UPPER = jnp.float32
NEVER = -1e30
SLOT = 16
VMEM_LIMIT = 56 * 1024 * 1024


def dot(left, right, dims):
    return lax.dot_general(left, right, ((dims[0], dims[1]), ((), ())), preferred_element_type=UPPER)


def mm(left, right):
    return dot(left, right, ((1,), (0,)))


def mm_nt(left, right):
    return dot(left, right, ((1,), (1,)))


def mm_tn(left, right):
    return dot(left, right, ((0,), (0,)))


def normalize(values):
    center = values - jnp.mean(values, -1, keepdims=True)
    inverse = lax.rsqrt(jnp.mean(center * center, -1, keepdims=True) + EPSILON)
    return (center * inverse, inverse)


def norm_back(grad_normed, normed, inverse):
    mean_grad = jnp.mean(grad_normed, -1, keepdims=True)
    mean_proj = jnp.mean(grad_normed * normed, -1, keepdims=True)
    return inverse * (grad_normed - mean_grad - normed * mean_proj)


class Moves:
    def __init__(self, dp_size):
        self.dp_size = dp_size
        self.staged = dp_size == 16
        self.dp = lax.axis_index("dp")
        self.mp = lax.axis_index("mp")
        if self.staged:
            self.blocks = (4, 4)
            z, here = self.dp // 4, self.dp % 4
            came = [((z - k) % 4) * 4 + (here ^ b) for b in range(4) for k in range(4)]
            goes = [((z + k) % 4) * 4 + (here ^ b) for b in range(4) for k in range(4)]
        else:
            self.blocks = (1, 1)
            came = goes = [self.dp * 0]
        self.came_at, self.goes_at, self.chips_at = 2, 2 + len(came), 2
        table = [self.mp, self.dp] + came + goes
        if not self.staged:
            self.chips_at = len(table)
            table += [self.dp * 0 + chip for chip in range(dp_size)]
        self.info = jnp.stack(table).astype(jnp.int32)

    def swap(self, value):
        return lax.ppermute(value, "mp", [(0, 1), (1, 0)])

    def in_order(self, own, other, axis=0):
        return jnp.where(
            self.mp == 0,
            jnp.concatenate([own, other], axis),
            jnp.concatenate([other, own], axis),
        )

    def flip(self, value, bits):
        return lax.ppermute(value, "dp", [(d, d ^ bits) for d in range(16)])

    def turn(self, value, step):
        return lax.ppermute(value, "dp", [(d, (d + 4 * step) % 16) for d in range(16)])

    def line(self, value):
        if not self.staged:
            return value
        return jnp.stack([value] + [self.turn(value, step) for step in (1, 2, 3)])

    def spread(self, line, chips=False):
        if not self.staged:
            value = lax.all_gather(line, "dp", axis=0, tiled=not chips)
            return [value if chips else value[None]]
        return [line] + [self.flip(line, bits) for bits in (1, 2, 3)]

    def meet(self, parts):
        if not self.staged:
            return parts
        return [parts[0]] + [self.flip(parts[bits], bits) for bits in (1, 2, 3)]

    def fold(self, terms):
        if not self.staged:
            return terms
        size = terms[0].shape[0] // 4
        sums = [
            sum(term[step * size : (step + 1) * size].astype(UPPER) for term in terms)
            for step in range(4)
        ]
        return sums[:1] + [part.astype(terms[0].dtype) for part in sums[1:]]

    def finish(self, sums):
        if not self.staged:
            return lax.psum_scatter(
                sums[0].astype(UPPER), "dp", scatter_dimension=0, tiled=True
            )
        total = sums[0]
        for step in (1, 2, 3):
            total = total + self.turn(sums[step], step).astype(UPPER)
        return total

    def square_to_line(self, value):
        if not self.staged:
            return value
        rows, columns = value.shape
        groups = [[4 * z + here for here in range(4)] for z in range(4)]
        return lax.all_to_all(
            value.reshape(4, rows // 4, columns), "dp", 0, 0, axis_index_groups=groups, tiled=True
        )

    def square_sums(self, value):
        if not self.staged:
            return value
        _, rows, columns = value.shape
        total = sum(value[number].astype(UPPER) for number in range(4)).astype(value.dtype)
        return total.reshape(4, rows // 4, columns)

    def line_to_own(self, value):
        if not self.staged:
            return lax.psum_scatter(value.astype(UPPER), "dp", scatter_dimension=0, tiled=True)
        groups = [[4 * z + here for z in range(4)] for here in range(4)]
        value = lax.all_to_all(value, "dp", 0, 0, axis_index_groups=groups, tiled=True)
        return sum(value[number].astype(UPPER) for number in range(4))

    def sum_cores(self, parts, other):
        came = self.swap(other)
        size = parts[0].shape[0]
        return [
            (part.astype(UPPER) + came[b * size : (b + 1) * size].astype(UPPER)).astype(LOWER)
            for b, part in enumerate(parts)
        ]


def wait_for(value, *others):
    return lax.optimization_barrier((value, *others))[0]


ANY = pl.BlockSpec(memory_space=pl.ANY)


def whole(shape):
    return pl.BlockSpec(shape, lambda *_: (0,) * len(shape))


def call(kernel, info, inputs, outputs, scratch=(), grid=(1,), flops=0, moved=0, name=None, after=(), aliased=()):
    skipped = list(aliased) + list(after)

    def inner(info_ref, *refs):
        kernel(info_ref, *refs[len(skipped) :])

    inputs = [(array, ANY) for array in skipped] + inputs
    return pl.pallas_call(
        inner,
        input_output_aliases={1 + number: number for number in range(len(aliased))},
        out_shape=[jax.ShapeDtypeStruct(shape, kind) for shape, kind, _ in outputs],
        grid_spec=pltpu.PrefetchScalarGridSpec(
            num_scalar_prefetch=1,
            grid=grid,
            in_specs=[spec for _, spec in inputs],
            out_specs=[spec for _, _, spec in outputs],
            scratch_shapes=list(scratch),
        ),
        compiler_params=pltpu.CompilerParams(
            dimension_semantics=("arbitrary",) * len(grid), vmem_limit_bytes=VMEM_LIMIT
        ),
        cost_estimate=pl.CostEstimate(flops=flops, bytes_accessed=moved, transcendentals=0),
        name=name,
    )(info, *[array for array, _ in inputs])


def bring(info, at, pieces, parts, sems, take=None):
    copies = []
    for b, piece in enumerate(pieces):
        count, rows, _ = piece.shape
        rows = take or rows
        for k in range(count):
            number = b * count + k
            start = pl.multiple_of(info[at + number] * rows, 16)
            for p, (target, column, source, columns) in enumerate(parts):
                copy = pltpu.make_async_copy(
                    piece.at[k, pl.ds(0, rows), pl.ds(source, columns)],
                    target.at[pl.ds(start, rows), pl.ds(column, columns)],
                    sems.at[number * len(parts) + p],
                )
                copy.start()
                copies.append(copy)
    return copies


def place(info, at, full, targets, column, columns, single=False):
    if single:
        (target,) = targets
    nb, nk = (4, 4) if at > 3 else (1, 1)
    rows = full.shape[0] // (nb * nk)
    for b in range(nb):
        for k in range(nk):
            start = pl.multiple_of(info[at + b * nk + k] * rows, 16)
            value = full[pl.ds(start, rows), :]
            if single:
                target[(b * nk + k) * rows : (b * nk + k + 1) * rows, column : column + columns] = value
            else:
                targets[b][k * rows : (k + 1) * rows, column : column + columns] = value


def place_square(staged, full, target, column, columns):
    if not staged:
        target[:, column : column + columns] = full[...]
        return
    rows = full.shape[0] // 16
    for here in range(4):
        for z in range(4):
            target[(here * 4 + z) * rows : (here * 4 + z + 1) * rows, column : column + columns] = full[
                (z * 4 + here) * rows : (z * 4 + here + 1) * rows, :
            ]


def grouped_rows(tokens, latents):
    pad = jnp.zeros((SLOT - latents.shape[0], latents.shape[1]), UPPER)
    return jnp.concatenate([tokens, latents, pad], 0)


def attention_forward(move, first, count, tokens, latents, mod, own_w, other_w, sizes):
    group_len, lat_count, features, half = sizes
    groups = tokens.shape[0] // group_len
    length = group_len + SLOT
    real = group_len + lat_count
    heads = half // HD
    np_ = len(own_w)

    def kernel(info, tok, lat, mod_ref, *refs):
        own, other = refs[:np_], refs[np_ : 2 * np_]
        after, lat_one, triple_ref, stats, mixed_ref, att_ref = refs[2 * np_ : 2 * np_ + 6]
        w_own, w_other, w_out, sems = refs[2 * np_ + 6 :]

        @pl.when(pl.program_id(0) == 0)
        def _():
            number = sems.shape[0] // 2
            copies = bring(
                info, move.came_at, own,
                [(w_own, 0, 0, 3 * half), (w_out, 0, 3 * half, half)], sems.at[pl.ds(0, number)],
            ) + bring(
                info, move.came_at, other,
                [(w_other, 0, 0, 3 * half), (w_out, half, 3 * half, half)],
                sems.at[pl.ds(number, number)],
            )
            for copy in copies:
                copy.wait()

        rows = grouped_rows(tok[...], lat[...])
        shift, scale, gate = [mod_ref[0, :, i * features : (i + 1) * features] for i in range(3)]
        normed, _ = normalize(rows)
        inputs = (normed * (1.0 + scale) + shift).astype(LOWER)
        for side, weight in ((0, w_own), (1, w_other)):
            triple = mm(inputs, weight[...]).astype(LOWER)
            triple_ref[:, side * 3 * half : (side + 1) * 3 * half] = triple
            pair = []
            for head in range(heads):
                query, key, value = [
                    triple[:, kind * half + head * HD : kind * half + (head + 1) * HD]
                    for kind in range(3)
                ]
                scores = mm_nt(key, query) * SCALING
                scores = jnp.concatenate(
                    [scores[:real], jnp.full((length - real, length), NEVER, UPPER)], 0
                )
                peak = jnp.max(scores, 0, keepdims=True)
                weights = jnp.exp(scores - peak)
                total = jnp.sum(weights, 0, keepdims=True)
                stats[0, side * heads + head : side * heads + head + 1, :] = peak + jnp.log(total)
                weights = (weights * (1.0 / total)).astype(LOWER)
                pair.append(mm_tn(weights, value).astype(LOWER))
                if len(pair) == 2:
                    at = side * half + (head - 1) * HD
                    mixed_ref[:, at : at + 2 * HD] = jnp.concatenate(pair, 1)
                    pair = []
        attended = mm_nt(mixed_ref[...], w_out[...])
        att_ref[...] = attended.astype(LOWER)
        result = rows + gate * attended
        after[...] = result[:group_len]
        lat_one[...] = result[group_len:real]

    at = lambda g, info: (info[0] * groups // 2 + first + g, 0)
    sems = 2 * np_ * own_w[0].shape[0]
    return call(
        kernel,
        move.info,
        [
            (tokens, pl.BlockSpec((group_len, features), at)),
            (latents, pl.BlockSpec((lat_count, features), at)),
            (mod, pl.BlockSpec((1, 1, 3 * features), lambda g, info: (first + g, 0, 0))),
        ]
        + [(piece, ANY) for piece in own_w + other_w],
        [
            ((count * group_len, features), UPPER, pl.BlockSpec((group_len, features), lambda g, info: (g, 0))),
            ((count * lat_count, features), UPPER, pl.BlockSpec((lat_count, features), lambda g, info: (g, 0))),
            ((count * length, 6 * half), LOWER, pl.BlockSpec((length, 6 * half), lambda g, info: (g, 0))),
            ((count, 2 * heads, length), UPPER, pl.BlockSpec((1, 2 * heads, length), lambda g, info: (g, 0, 0))),
            ((count * length, features), LOWER, pl.BlockSpec((length, features), lambda g, info: (g, 0))),
            ((count * length, features), LOWER, pl.BlockSpec((length, features), lambda g, info: (g, 0))),
        ],
        [
            pltpu.VMEM((features, 3 * half), LOWER),
            pltpu.VMEM((features, 3 * half), LOWER),
            pltpu.VMEM((features, 2 * half), LOWER),
            pltpu.SemaphoreType.DMA((2 * sems,)),
        ],
        grid=(count,),
        flops=count * length * features * features * 8 * 2,
        moved=count * 4_000_000,
        name="attention_forward",
    )


def attention_entry(
    move, lat_own, lat_came, lat_one, grad_two, gain, mod, grad_tok, attended, sizes, after=()
):
    group_len, lat_count, features, half = sizes
    count = lat_one.shape[0] // lat_count
    length = group_len + SLOT

    def kernel(info, own, came, lat, two, gain_ref, mod_ref, gtok, att, grad_lat, grad_att, vec):
        normed, inverse = normalize(lat[...])
        into = two[...] + norm_back((own[...] + came[...]) * gain_ref[...], normed, inverse)
        grad_lat[...] = into
        rows = grouped_rows(gtok[...], into)
        vec[0] = jnp.sum(rows * att[...].astype(UPPER), 0, keepdims=True)
        grad_att[...] = (mod_ref[0, :, 2 * features :] * rows).astype(LOWER)

    row = lambda size, columns: pl.BlockSpec((size, columns), lambda g, info: (g, 0))
    return call(
        kernel,
        move.info,
        [(value, row(lat_count, features)) for value in (lat_own, lat_came, lat_one, grad_two)]
        + [
            (gain, whole(gain.shape)),
            (mod, pl.BlockSpec((1, 1, 3 * features), lambda g, info: (g, 0, 0))),
            (grad_tok, row(group_len, features)),
            (attended, row(length, features)),
        ],
        [
            ((count * lat_count, features), UPPER, row(lat_count, features)),
            ((count * length, features), LOWER, row(length, features)),
            ((count, 1, features), UPPER, pl.BlockSpec((1, 1, features), lambda g, info: (g, 0, 0))),
        ],
        grid=(count,),
        flops=count * length * features * 10,
        moved=count * 2_500_000,
        name="attention_entry",
        after=after,
    )


def attention_backward(
    move, first, count, tokens, latents, mod, grad_tok, grad_lat, grad_att, saved, own_w, other_w, sizes, before=(), after=()
):
    group_len, lat_count, features, half = sizes
    groups = tokens.shape[0] // group_len
    mine = groups // 2
    length = group_len + SLOT
    real = group_len + lat_count
    heads = half // HD
    np_ = len(own_w)
    triple_all, stats_all = saved

    def kernel(info, tok, lat, mod_ref, gtok, glat, gatt, triple, stats, *refs):
        own, other = refs[:np_], refs[np_ : 2 * np_]
        out_tok, out_lat, in_ref, tri_ref, vec_ref, full = refs[2 * np_ : 2 * np_ + 6]
        w_in, w_out, sems = refs[2 * np_ + 6 :]

        @pl.when(pl.program_id(0) == 0)
        def _():
            number = sems.shape[0] // 2
            copies = []
            for side, pieces in ((0, own), (1, other)):
                parts = [(w_in, side * 3 * half, 0, 3 * half), (w_out, side * half, 3 * half, half)]
                copies += bring(info, move.came_at, pieces, parts, sems.at[pl.ds(side * number, number)])
            for copy in copies:
                copy.wait()

        rows = grouped_rows(tok[...], lat[...])
        shift, scale = [mod_ref[0, :, i * features : (i + 1) * features] for i in range(2)]
        normed, inverse = normalize(rows)
        in_ref[...] = (normed * (1.0 + scale) + shift).astype(LOWER)
        grad_mixed_all = mm(gatt[...], w_out[...]).astype(LOWER)
        for side in range(2):
            pairs = ([], [], [])
            for head in range(heads):
                base = side * 3 * half + head * HD
                query, key, value = [
                    triple[:, base + kind * half : base + kind * half + HD] for kind in range(3)
                ]
                at = side * half + head * HD
                grad_mixed = grad_mixed_all[:, at : at + HD]
                scores = mm_nt(key, query) * SCALING
                scores = jnp.concatenate(
                    [scores[:real], jnp.full((length - real, length), NEVER, UPPER)], 0
                )
                weights = jnp.exp(scores - stats[0, side * heads + head : side * heads + head + 1, :])
                grad_weights = mm_nt(value, grad_mixed)
                delta = jnp.sum(grad_weights * weights, 0, keepdims=True)
                grad_scores = (weights * (grad_weights - delta)).astype(LOWER)
                pairs[0].append((mm_tn(grad_scores, key) * SCALING).astype(LOWER))
                pairs[1].append((mm(grad_scores, query) * SCALING).astype(LOWER))
                pairs[2].append(mm(weights.astype(LOWER), grad_mixed).astype(LOWER))
                if head % 2:
                    for kind in range(3):
                        at = base + kind * half - HD
                        tri_ref[:, at : at + 2 * HD] = jnp.concatenate(pairs[kind][-2:], 1)
        grad_inputs = mm_nt(tri_ref[...], w_in[...])
        vec_ref[0, 0:1, :] = jnp.sum(grad_inputs, 0, keepdims=True)
        vec_ref[0, 1:2, :] = jnp.sum(grad_inputs * normed, 0, keepdims=True)
        result = grouped_rows(gtok[...], glat[...]) + norm_back(
            grad_inputs * (1.0 + scale), normed, inverse
        )
        out_tok[...] = result[:group_len]
        full[...] = result[:group_len]
        out_lat[...] = result[group_len:real]

    at = lambda g, info: (info[0] * mine + first + g, 0)
    row = lambda size, columns: pl.BlockSpec((size, columns), lambda g, info: (first + g, 0))
    vector = lambda n, size: pl.BlockSpec((1, n, size), lambda g, info: (first + g, 0, 0))
    return call(
        kernel,
        move.info,
        [
            (tokens, pl.BlockSpec((group_len, features), at)),
            (latents, pl.BlockSpec((lat_count, features), at)),
            (mod, vector(1, 3 * features)),
            (grad_tok, row(group_len, features)),
            (grad_lat, row(lat_count, features)),
            (grad_att, row(length, features)),
            (triple_all, row(length, 6 * half)),
            (stats_all, vector(2 * heads, length)),
        ]
        + [(piece, ANY) for piece in own_w + other_w],
        [
            ((mine * group_len, features), UPPER, row(group_len, features)),
            ((mine * lat_count, features), UPPER, row(lat_count, features)),
            ((mine * length, features), LOWER, row(length, features)),
            ((mine * length, 6 * half), LOWER, row(length, 6 * half)),
            ((mine, 2, features), UPPER, vector(2, features)),
            (tokens.shape, UPPER, pl.BlockSpec((group_len, features), at)),
        ],
        [
            pltpu.VMEM((features, 6 * half), LOWER),
            pltpu.VMEM((features, 2 * half), LOWER),
            pltpu.SemaphoreType.DMA((4 * np_ * own_w[0].shape[0],)),
        ],
        grid=(count,),
        flops=count * length * features * features * 20,
        moved=count * 5_000_000,
        name="attention_backward",
        aliased=before,
        after=after,
    )


def attention_gradients(move, side, inputs, triples, grad_att, mixed, half, came=(), after=()):
    total, features = inputs.shape
    nb, nk = move.blocks
    columns = 4 * half

    def kernel(info, in_ref, tri_ref, att_ref, mix_ref, *refs):
        first = mm(jnp.transpose(in_ref[...]), tri_ref[...])
        second = mm(jnp.transpose(att_ref[...]), mix_ref[...])
        if side == 1:
            refs[0][:, : 3 * half] = first.astype(LOWER)
            refs[0][:, 3 * half :] = second.astype(LOWER)
        else:
            other, grads, square = refs[0], refs[1:-1], refs[-1]
            square[:, : 3 * half] = (first + other[:, : 3 * half].astype(UPPER)).astype(LOWER)
            square[:, 3 * half :] = (second + other[:, 3 * half :].astype(UPPER)).astype(LOWER)
            place(info, move.goes_at, square, grads, 0, columns)

    rows = [features // nb] * nb if side == 0 else [features]
    return call(
        kernel,
        move.info,
        [
            (inputs, whole(inputs.shape)),
            (triples, pl.BlockSpec((total, 3 * half), lambda i, info: (0, side))),
            (grad_att, whole(grad_att.shape)),
            (mixed, pl.BlockSpec((total, half), lambda i, info: (0, side))),
        ]
        + [(part, whole(part.shape)) for part in came],
        [((size, columns), LOWER, whole((size, columns))) for size in rows],
        [pltpu.VMEM((features, columns), LOWER)] if side == 0 else [],
        flops=total * features * columns * 2,
        moved=total * (features + columns) * 2,
        name="attention_gradients",
        after=after,
    )


ROOT = 0.7978845608028654
CUBE = 0.044715


def feed_forward(rows, grad_result, shift, scale, gate, w_up, w_down, hidden_ref, upward_ref, step=768):
    normed, inverse = normalize(rows)
    inputs = (normed * (1.0 + scale) + shift).astype(LOWER)
    grad_narrow = (gate * grad_result).astype(LOWER)
    narrowed = grad_inputs = 0.0
    for start in range(0, w_up.shape[1], step):
        units = slice(start, start + step)
        upward = mm(inputs, w_up[:, units])
        square = upward * upward
        bend = jnp.tanh(upward * (ROOT + (ROOT * CUBE) * square))
        half_up = 0.5 * upward
        hidden = (half_up * (1.0 + bend)).astype(LOWER)
        slope = 0.5 * (1.0 + bend) + half_up * (1.0 - bend * bend) * (
            ROOT + (3.0 * ROOT * CUBE) * square
        )
        grad_upward = (mm(grad_narrow, w_down[:, units]) * slope).astype(LOWER)
        hidden_ref[:, units] = hidden
        upward_ref[:, units] = grad_upward
        narrowed = narrowed + mm_nt(hidden, w_down[:, units])
        grad_inputs = grad_inputs + mm_nt(grad_upward, w_up[:, units])
    result = rows + gate * narrowed
    grad_rows = grad_result + norm_back(grad_inputs * (1.0 + scale), normed, inverse)
    return result, grad_rows, inputs, grad_narrow, (
        grad_inputs,
        grad_inputs * normed,
        grad_result * narrowed,
    )


def bring_wide(wide, w_up, w_down, sems):
    units = w_up.shape[1] // 2
    count, rows, _ = wide.shape
    copies = []
    for entry in range(count):
        at = pl.ds(entry // 2 * rows, rows)
        for which, target in enumerate((w_up, w_down)):
            copies.append(
                pltpu.make_async_copy(
                    wide.at[entry, :, pl.ds(which * units, units)],
                    target.at[at, pl.ds(entry % 2 * units, units)],
                    sems.at[2 * entry + which],
                )
            )
    for copy in copies:
        copy.start()
    for copy in copies:
        copy.wait()


def token_feed_forward(move, first, count, rows, cotangent, mod, wide_w, sizes, before=(), after=()):
    group_len, lat_count, features, half = sizes
    groups = cotangent.shape[0] // group_len
    units = wide_w.shape[2] // 2

    def kernel(info, row_ref, cot, mod_ref, *refs):
        wide = refs[0]
        result, grad, inputs_ref, narrow_ref, hidden_ref, upward_ref, vec, full = refs[1:9]
        w_up, w_down, sems = refs[9:]

        @pl.when(pl.program_id(0) == 0)
        def _():
            bring_wide(wide, w_up, w_down, sems)

        shift, scale, gate = [mod_ref[0, :, i * features : (i + 1) * features] for i in range(3)]
        out, grad_rows, inputs, narrow, terms = feed_forward(
            row_ref[...], cot[...], shift, scale, gate, w_up, w_down, hidden_ref, upward_ref
        )
        result[...] = out
        full[...] = out
        grad[...] = grad_rows
        inputs_ref[...] = jnp.transpose(inputs)
        narrow_ref[...] = jnp.transpose(narrow)
        for number, term in enumerate(terms):
            vec[0, number : number + 1, :] = jnp.sum(term, 0, keepdims=True)

    at = pl.BlockSpec((group_len, features), lambda g, info: (info[0] * groups // 2 + first + g, 0))
    turned = pl.BlockSpec((features, group_len), lambda g, info: (0, first + g))
    row = lambda columns: pl.BlockSpec((group_len, columns), lambda g, info: (first + g, 0))
    total = rows.shape[0]
    return call(
        kernel,
        move.info,
        [
            (rows, row(features)),
            (
                cotangent,
                at,
            ),
            (mod, pl.BlockSpec((1, 1, 3 * features), lambda g, info: (first + g, 0, 0))),
        ]
        + [(wide_w, ANY)],
        [
            ((total, features), UPPER, row(features)),
            ((total, features), UPPER, row(features)),
            ((features, total), LOWER, turned),
            ((features, total), LOWER, turned),
            ((total, 2 * units), LOWER, row(2 * units)),
            ((total, 2 * units), LOWER, row(2 * units)),
            ((groups // 2, 3, features), UPPER, pl.BlockSpec((1, 3, features), lambda g, info: (first + g, 0, 0))),
            (cotangent.shape, UPPER, at),
        ],
        [
            pltpu.VMEM((features, 2 * units), LOWER),
            pltpu.VMEM((features, 2 * units), LOWER),
            pltpu.SemaphoreType.DMA((2 * wide_w.shape[0],)),
        ],
        grid=(count,),
        flops=count * group_len * features * units * 16,
        moved=count * 8_000_000,
        name="token_feed_forward",
        aliased=before,
        after=after,
    )


def latent_feed_forward(move, lat_one, branch, came, cotangent, mod, wide_w, sizes, after=()):
    group_len, lat_count, features, half = sizes
    rows_n = lat_one.shape[0]
    count = rows_n // lat_count
    units = wide_w.shape[2] // 2

    def kernel(info, one, own, other, cot, mod_ref, *refs):
        wide = refs[0]
        result, grad, inputs_ref, narrow_ref, hidden_ref, upward_ref, vec = refs[1:8]
        w_up, w_down, sems = refs[8:]
        bring_wide(wide, w_up, w_down, sems)
        vectors = [
            jnp.concatenate(
                [
                    jnp.broadcast_to(mod_ref[g, :, i * features : (i + 1) * features], (lat_count, features))
                    for g in range(count)
                ],
                0,
            )
            for i in range(3)
        ]
        rows = one[...] + own[...] + other[...]
        out, grad_rows, inputs, narrow, terms = feed_forward(
            rows, cot[...], *vectors, w_up, w_down, hidden_ref, upward_ref
        )
        result[...] = out
        grad[...] = grad_rows
        inputs_ref[...] = inputs
        narrow_ref[...] = narrow
        for number, term in enumerate(terms):
            for g in range(count):
                vec[g, number : number + 1, :] = jnp.sum(
                    term[g * lat_count : (g + 1) * lat_count], 0, keepdims=True
                )

    rows_f = (rows_n, features)
    return call(
        kernel,
        move.info,
        [
            (lat_one, whole(rows_f)),
            (branch, whole(rows_f)),
            (came, whole(rows_f)),
            (cotangent, pl.BlockSpec(rows_f, lambda i, info: (info[0], 0))),
            (mod, whole(mod.shape)),
        ]
        + [(wide_w, ANY)],
        [
            (rows_f, UPPER, whole(rows_f)),
            (rows_f, UPPER, whole(rows_f)),
            (rows_f, LOWER, whole(rows_f)),
            (rows_f, LOWER, whole(rows_f)),
            ((rows_n, 2 * units), LOWER, whole((rows_n, 2 * units))),
            ((rows_n, 2 * units), LOWER, whole((rows_n, 2 * units))),
            ((count, 3, features), UPPER, whole((count, 3, features))),
        ],
        [
            pltpu.VMEM((features, 2 * units), LOWER),
            pltpu.VMEM((features, 2 * units), LOWER),
            pltpu.SemaphoreType.DMA((2 * wide_w.shape[0],)),
        ],
        flops=rows_n * features * units * 64,
        moved=12_000_000,
        name="latent_feed_forward",
        after=after,
    )


def wide_gradients(move, at, left, right, lat_left, lat_right, before=(), after=(), tile=768):
    features, total = left.shape
    units = right.shape[1] // 2
    tiles = units // tile

    def kernel(info, left_ref, right_ref, lat_l, lat_r, out):
        acc = mm_tn(lat_l[...], lat_r[...]) + mm(left_ref[...], right_ref[...])
        out[...] = acc.astype(LOWER)

    columns = lambda rows: pl.BlockSpec((rows, tile), lambda s, info: (0, s))
    return call(
        kernel,
        move.info,
        [
            (left, whole(left.shape)),
            (right, columns(total)),
            (lat_left, whole(lat_left.shape)),
            (lat_right, columns(lat_right.shape[0])),
        ],
        [
            (
                (2 * features, 2 * units),
                LOWER,
                pl.BlockSpec((features, tile), lambda s, info: (s // tiles, at * tiles + s % tiles)),
            )
        ],
        grid=(2 * tiles,),
        flops=total * features * units * 4,
        moved=total * units * 4 + features * units * 4,
        name="wide_gradients",
        aliased=before,
        after=after,
    )[0]


def modulation_terms(move, vectors, modulator, bias, middle):
    shard, width = modulator.shape
    size = middle // 2
    nb = len(vectors)
    count = vectors[0].shape[0]
    rows = vectors[0].shape[1]
    chips = count * rows // SLOT
    features = vectors[0].shape[2]

    def kernel(info, *refs):
        pieces = refs[:nb]
        mods, biases = refs[nb : nb + 2], refs[nb + 2 : nb + 4]
        outs = refs[nb + 4 :]
        terms, picked, gain = outs[:nb], outs[nb : 2 * nb], outs[2 * nb]
        shape = (features, shard)
        select = lax.broadcasted_iota(jnp.int32, shape, 0) == (
            lax.broadcasted_iota(jnp.int32, shape, 1) + info[1] * shard
        )
        select = jnp.where(select, 1.0, 0.0).astype(LOWER)
        gains = jnp.zeros((1, features), UPPER)
        for b in range(nb):
            value = pieces[b][...].reshape(chips * SLOT, features)
            gains = gains + jnp.sum(
                value.astype(UPPER).reshape(chips, SLOT, features)[:, 8:9, :], 0
            )
            mine = mm(value, select)
            picked[b][...] = jnp.concatenate(
                [
                    jnp.where(
                        info[0] == 0,
                        mine[k * SLOT : k * SLOT + 4],
                        mine[k * SLOT + 4 : k * SLOT + 8],
                    )
                    for k in range(chips)
                ],
                0,
            )
            for part in range(2):
                product = mm(mine.astype(LOWER), mods[part][...].astype(LOWER)) + biases[part][...]
                product = product.reshape(chips, SLOT, size)
                for k in range(chips):
                    where = (chips - k) % chips if nb > 1 else k
                    terms[b][where, :, part * size : (part + 1) * size] = product[k, :8]
        gain[...] = gains

    columns = lambda rows_, part: pl.BlockSpec((rows_, size), lambda i, info: (0, 2 * part + info[0]))
    return call(
        kernel,
        move.info,
        [(piece, whole(piece.shape)) for piece in vectors]
        + [(modulator, columns(shard, 0)), (modulator, columns(shard, 1))]
        + [(bias, columns(1, 0)), (bias, columns(1, 1))],
        [((chips, 8, 2 * size), UPPER, whole((chips, 8, 2 * size)))] * nb
        + [((chips * 4, shard), UPPER, whole((chips * 4, shard)))] * nb
        + [((1, features), UPPER, whole((1, features)))],
        flops=10_000_000,
        moved=3_000_000,
        name="modulation_terms",
    )


def modulation_gradients(move, picked, grads, modulator, dp_size, after=()):
    shard, width = modulator.shape
    features = width // 6
    nb = len(grads)
    chips = dp_size // nb
    own = 4

    def kernel(info, *refs):
        picks, parts = refs[:nb], refs[nb : 2 * nb]
        mod_ref, out, terms = refs[2 * nb :]
        products = [jnp.zeros((chips * own, shard), UPPER) for _ in range(nb)]
        for i in range(6):
            at = slice(i * features, (i + 1) * features)
            weight = mod_ref[:, at].astype(LOWER)
            total = jnp.zeros((shard, features), UPPER)
            sums = jnp.zeros((1, features), UPPER)
            for b in range(nb):
                value = parts[b][:, i // 2 * 8 : i // 2 * 8 + 8, :].astype(UPPER)
                value = jnp.concatenate(
                    [value[k, i % 2 * own : (i % 2 + 1) * own] for k in range(chips)], 0
                )
                sums = sums + jnp.sum(value, 0, keepdims=True)
                value = value.astype(LOWER)
                total = total + mm_tn(picks[b][...].astype(LOWER), value)
                products[b] = products[b] + mm_nt(value, weight)
            out[:shard, at] = total
            extra = jnp.zeros((1, features), UPPER)
            if i == 0:
                for b in range(nb):
                    for k in range(chips):
                        extra = extra + jnp.sum(parts[b][k, 24:32, :].astype(UPPER), 0, keepdims=True)
            out[shard:, at] = jnp.concatenate(
                [sums, extra, jnp.zeros((6, features), UPPER)], 0
            )
        for b in range(nb):
            for k in range(chips):
                terms[info[move.chips_at + b * chips + k]] = products[b][k * own : (k + 1) * own]

    return call(
        kernel,
        move.info,
        [(piece, whole(piece.shape)) for piece in picked]
        + [(piece, whole(piece.shape)) for piece in grads]
        + [(modulator, whole(modulator.shape))],
        [
            ((shard + 8, width), UPPER, whole((shard + 8, width))),
            ((dp_size, own, shard), UPPER, whole((dp_size, own, shard))),
        ],
        flops=10_000_000,
        moved=3_000_000,
        name="modulation_gradients",
        after=after,
    )


def latent_project(move, own, other, gain, weights, half):
    rows_n, features = own.shape
    np_ = len(weights)

    def kernel(info, own_ref, other_ref, gain_ref, *refs):
        pieces = refs[:np_]
        triple, lat_in, weight, rows, sems = refs[np_:]
        copies = bring(info, move.came_at, pieces, [(weight, 0, 0, 4 * half)], sems)
        here = pl.multiple_of(info[0] * rows_n, rows_n)
        there = pl.multiple_of((1 - info[0]) * rows_n, rows_n)
        rows[pl.ds(here, rows_n), :] = own_ref[...]
        rows[pl.ds(there, rows_n), :] = other_ref[...]
        normed, _ = normalize(rows[...])
        inputs = (normed * gain_ref[...]).astype(LOWER)
        lat_in[...] = inputs
        for copy in copies:
            copy.wait()
        triple[...] = mm(inputs, weight[:, : 3 * half]).astype(LOWER)

    total = 2 * rows_n
    shapes = [(total, 3 * half), (total, features), (features, 4 * half)]
    return call(
        kernel,
        move.info,
        [(own, whole(own.shape)), (other, whole(own.shape)), (gain, whole(gain.shape))]
        + [(piece, ANY) for piece in weights],
        [(shape, LOWER, whole(shape)) for shape in shapes],
        [
            pltpu.VMEM((total, features), UPPER),
            pltpu.SemaphoreType.DMA((np_ * weights[0].shape[0],)),
        ],
        flops=500_000_000,
        moved=6_000_000,
        name="latent_project",
    )


def allowed_pairs(info, own_image, image, keep, own_keep=None):
    count, total = own_image.shape[0], image.shape[1]
    shape = (count, total)
    itself = lax.broadcasted_iota(jnp.int32, shape, 1) == (
        lax.broadcasted_iota(jnp.int32, shape, 0) + info[1] * count
    )
    kept = (keep if own_keep is None else own_keep) == 1
    return (own_image == image) & (kept | itself)


def split_rows(info, full, own, other):
    rows = own.shape[0]
    own[...] = full[pl.ds(pl.multiple_of(info[0] * rows, rows), rows), :]
    other[...] = full[pl.ds(pl.multiple_of((1 - info[0]) * rows, rows), rows), :]


def latent_forward(move, query, key_values, weights, masks, half, features, after=()):
    count = query.shape[0]
    np_ = len(key_values)
    total = np_ * key_values[0].shape[0] * count
    heads = half // HD

    def kernel(info, query_ref, weight, own_image, image, keep, *refs):
        pieces = refs[:np_]
        mixed, stats, own, other, all_kv, full, sems = refs[np_:]
        copies = bring(info, move.chips_at, pieces, [(all_kv, 0, half, 2 * half)], sems)
        allowed = allowed_pairs(info, own_image[...], image[...], keep[...])
        for copy in copies:
            copy.wait()
        lane = lax.broadcasted_iota(jnp.int32, (count, 128), 1)
        logs = jnp.zeros((count, 128), UPPER)
        outs = []
        for head in range(heads):
            at = slice(head * HD, (head + 1) * HD)
            scores = mm_nt(query_ref[:, at], all_kv[:, at]) * SCALING
            scores = jnp.where(allowed, scores, NEVER)
            peak = jnp.max(scores, 1, keepdims=True)
            weights_ = jnp.exp(scores - peak)
            sums = jnp.sum(weights_, 1, keepdims=True)
            logs = jnp.where(lane == head, peak + jnp.log(sums), logs)
            weights_ = (weights_ * (1.0 / sums)).astype(LOWER)
            outs.append(mm(weights_, all_kv[:, half + head * HD : half + (head + 1) * HD]).astype(LOWER))
        stats[...] = logs
        mixed[...] = jnp.concatenate(outs, 1)
        full[...] = mm_nt(mixed[...], weight[:, 3 * half :])
        split_rows(info, full, own, other)

    part = (count // 2, features)
    return call(
        kernel,
        move.info,
        [(query, whole(query.shape)), (weights, whole(weights.shape))]
        + [(mask, whole(mask.shape)) for mask in masks[:3]]
        + [(piece, ANY) for piece in key_values],
        [
            ((count, half), LOWER, whole((count, half))),
            ((count, 128), UPPER, whole((count, 128))),
            (part, UPPER, whole(part)),
            (part, UPPER, whole(part)),
        ],
        [
            pltpu.VMEM((total, 2 * half), LOWER),
            pltpu.VMEM((count, features), UPPER),
            pltpu.SemaphoreType.DMA((np_ * key_values[0].shape[0],)),
        ],
        flops=1_000_000_000,
        moved=6_000_000,
        name="latent_forward",
        after=after,
    )


def latent_backward(move, query, key_values, weights, masks, mixed, stats, grad_own, grad_other, half, features):
    count = query.shape[0]
    np_ = len(key_values)
    total = np_ * key_values[0].shape[0] * count
    heads = half // HD

    def kernel(info, query_ref, weight, own_image, image, keep, mixed_ref, stats_ref, own, other, *refs):
        pieces = refs[:np_]
        sent, grad_query, out_grad, all_kv, full, sems = refs[np_:]
        copies = bring(info, move.chips_at, pieces, [(all_kv, 0, half, 2 * half)], sems)
        allowed = allowed_pairs(info, own_image[...], image[...], keep[...])
        rows_n = own.shape[0]
        full[pl.ds(pl.multiple_of(info[0] * rows_n, rows_n), rows_n), :] = own[...]
        full[pl.ds(pl.multiple_of((1 - info[0]) * rows_n, rows_n), rows_n), :] = other[...]
        branch = full[...].astype(LOWER)
        grad_mixed = mm(branch, weight[:, 3 * half :]).astype(LOWER)
        out_grad[...] = mm_tn(branch, mixed_ref[...])
        sent[:, :half] = grad_mixed
        for copy in copies:
            copy.wait()
        lane = lax.broadcasted_iota(jnp.int32, (count, 128), 1)
        extra = jnp.zeros((count, 128), UPPER)
        outs = []
        for head in range(heads):
            at = slice(head * HD, (head + 1) * HD)
            scores = mm_nt(query_ref[:, at], all_kv[:, at]) * SCALING
            log_total = stats_ref[:, head : head + 1]
            weights_ = jnp.exp(jnp.where(allowed, scores - log_total, NEVER))
            grad_weights = mm_nt(grad_mixed[:, at], all_kv[:, half + head * HD : half + (head + 1) * HD])
            delta = jnp.sum(grad_weights * weights_, 1, keepdims=True)
            grad_scores = (weights_ * (grad_weights - delta)).astype(LOWER)
            outs.append((mm(grad_scores, all_kv[:, at]) * SCALING).astype(LOWER))
            for start, column in ((0, log_total), (3, delta)):
                high = column.astype(LOWER).astype(UPPER)
                middle = (column - high).astype(LOWER).astype(UPPER)
                low = column - high - middle
                for number, part in enumerate((high, middle, low)):
                    extra = jnp.where(lane == (start + number) * heads + head, part, extra)
        sent[:, half:] = extra.astype(LOWER)
        grad_query[...] = jnp.concatenate(outs, 1)

    return call(
        kernel,
        move.info,
        [(query, whole(query.shape)), (weights, whole(weights.shape))]
        + [(mask, whole(mask.shape)) for mask in masks[:3]]
        + [(value, whole(value.shape)) for value in (mixed, stats, grad_own, grad_other)]
        + [(piece, ANY) for piece in key_values],
        [
            ((count, half + 128), LOWER, whole((count, half + 128))),
            ((count, half), LOWER, whole((count, half))),
            ((features, half), UPPER, whole((features, half))),
        ],
        [
            pltpu.VMEM((total, 2 * half), LOWER),
            pltpu.VMEM((count, features), UPPER),
            pltpu.SemaphoreType.DMA((np_ * key_values[0].shape[0],)),
        ],
        flops=1_500_000_000,
        moved=6_000_000,
        name="latent_backward",
    )


def latent_sources(move, key_value, gathered, came, weights, masks, grad_query, lat_in, out_grad, lat_own, lat_other, gain, half, features, after=()):
    count = key_value.shape[0]
    np_ = len(came)
    total = np_ * came[0].shape[0] * count
    heads = half // HD
    nb, nk = move.blocks

    def kernel(info, kv, weight, own_image, image, own_keep, grad_query_ref, lat_in_ref, out_grad_ref, lat_o, lat_t, gain_ref, *refs):
        pieces, gathered_refs = refs[:np_], refs[np_ : 2 * np_]
        refs = refs[np_:]
        own, other, gain_rows = refs[np_ : np_ + 3]
        grads = refs[np_ + 3 : np_ + 4]
        all_q, full, rows, square, sems = refs[np_ + 4 :]
        number = sems.shape[0] // 2
        copies = bring(
            info, move.chips_at, pieces, [(all_q, half, 0, half + 128)], sems.at[pl.ds(0, number)]
        ) + bring(
            info, move.chips_at, gathered_refs, [(all_q, 0, 0, half)], sems.at[pl.ds(number, number)]
        )
        allowed = allowed_pairs(info, own_image[...], image[...], None, own_keep[...])
        for copy in copies:
            copy.wait()
        turned = jnp.transpose(all_q[:, 2 * half :].astype(UPPER))
        keys, values = [], []
        for head in range(heads):
            at = slice(head * HD, (head + 1) * HD)
            other_at = slice(half + head * HD, half + (head + 1) * HD)
            last_at = slice(2 * half + head * HD, 2 * half + (head + 1) * HD)
            log_total, delta = [
                sum(turned[(s + i) * heads + head : (s + i) * heads + head + 1] for i in range(3))
                for s in (0, 3)
            ]
            scores = mm_nt(kv[:, other_at], all_q[:, at]) * SCALING
            weights_ = jnp.exp(jnp.where(allowed, scores - log_total, NEVER))
            grad_weights = mm_nt(kv[:, last_at], all_q[:, other_at])
            grad_scores = (weights_ * (grad_weights - delta)).astype(LOWER)
            keys.append((mm(grad_scores, all_q[:, at]) * SCALING).astype(LOWER))
            values.append(mm(weights_.astype(LOWER), all_q[:, other_at]).astype(LOWER))
        triple = jnp.concatenate([grad_query_ref[...]] + keys + values, 1)
        full[...] = mm_nt(triple, weight[:, : 3 * half])
        split_rows(info, full, own, other)
        rows_n = lat_o.shape[0]
        rows[pl.ds(pl.multiple_of(info[0] * rows_n, rows_n), rows_n), :] = lat_o[...]
        rows[pl.ds(pl.multiple_of((1 - info[0]) * rows_n, rows_n), rows_n), :] = lat_t[...]
        normed, _ = normalize(rows[...])
        square[:, : 3 * half] = mm_tn(lat_in_ref[...], triple).astype(LOWER)
        square[:, 3 * half : 4 * half] = out_grad_ref[...].astype(LOWER)
        total_gain = jnp.sum(full[...] * normed, 0, keepdims=True)
        for number in range(3):
            part = total_gain.astype(LOWER).astype(UPPER)
            gain_rows[number : number + 1, :] = part
            total_gain = total_gain - part
        gain_rows[3:, :] = jnp.zeros((5, features), UPPER)
        place_square(move.staged, square, grads[0], 0, 4 * half)

    part = (count // 2, features)
    columns = 4 * half
    return call(
        kernel,
        move.info,
        [(key_value, whole(key_value.shape)), (weights, whole(weights.shape))]
        + [(mask, whole(mask.shape)) for mask in (masks[0], masks[1], masks[3])]
        + [
            (value, whole(value.shape))
            for value in (grad_query, lat_in, out_grad, lat_own, lat_other, gain)
        ]
        + [(piece, ANY) for piece in came + gathered],
        [(part, UPPER, whole(part))] * 2
        + [((8, features), UPPER, whole((8, features)))]
        + [((features, columns), LOWER, whole((features, columns)))],
        [
            pltpu.VMEM((total, 2 * half + 128), LOWER),
            pltpu.VMEM((count, features), UPPER),
            pltpu.VMEM((count, features), UPPER),
            pltpu.VMEM((features, columns), LOWER),
            pltpu.SemaphoreType.DMA((2 * np_ * came[0].shape[0],)),
        ],
        flops=2_000_000_000,
        moved=8_000_000,
        name="latent_sources",
        after=after,
    )


def fill(move, full, other, after=(), block=512):
    rows, features = other.shape
    block = min(block, rows)
    steps = rows // block

    def kernel(info, other_ref, out):
        out[...] = other_ref[...]

    return call(
        kernel,
        move.info,
        [(other, pl.BlockSpec((block, features), lambda i, info: (i, 0)))],
        [
            (
                full.shape,
                UPPER,
                pl.BlockSpec((block, features), lambda i, info: ((1 - info[0]) * steps + i, 0)),
            )
        ],
        grid=(steps,),
        moved=2 * rows * features * 4,
        name="fill",
        after=after,
        aliased=[full],
    )[0]


def make_body(dp_size):
    def body(
        tokens,
        latents,
        condition,
        modulator,
        offsets,
        local_qkv,
        local_out,
        global_qkv,
        global_out,
        latent_gain,
        up_weight,
        down_weight,
        group_image,
        latent_keep,
        token_cotangent,
        latent_cotangent,
    ):
        move = Moves(dp_size)
        mp, dp = move.mp, move.dp
        groups = condition.shape[0]
        own = groups // 2
        features = tokens.shape[1]
        group_len = tokens.shape[0] // groups
        lat_count = latents.shape[0] // groups
        shard, width = modulator.shape
        half = local_out.shape[1]
        units = up_weight.shape[1]
        middle = width // 2
        sizes = (group_len, lat_count, features, half)

        def mine(value):
            size = value.shape[0] // 2
            return lax.dynamic_slice_in_dim(value, mp * size, size, 0)

        def others(value):
            size = value.shape[0] // 2
            return lax.dynamic_slice_in_dim(value, (1 - mp) * size, size, 0)

        scaled = jax.nn.silu(condition).astype(LOWER)
        gain_row = lax.dynamic_update_slice(
            jnp.zeros((1, features), LOWER), latent_gain.astype(LOWER)[None], (0, dp * shard)
        )
        bias_row = lax.dynamic_update_slice(
            jnp.zeros((1, width), UPPER),
            offsets.astype(LOWER).astype(UPPER)[None],
            (0, dp * (width // dp_size)),
        )
        vectors = move.spread(
            move.line(
                jnp.concatenate(
                    [scaled, gain_row, jnp.zeros((SLOT - 1 - groups, features), LOWER)], 0
                )
            )
        )
        found = modulation_terms(move, vectors, modulator, bias_row, middle)
        nb = len(vectors)
        picked, gain = found[nb : 2 * nb], found[2 * nb]

        total = move.finish(
            move.fold(move.meet([term.reshape(-1, term.shape[2]) for term in found[:nb]]))
        )
        total, came = mine(total), move.swap(others(total))
        mod_one, mod_two = [
            move.in_order(total[:, part], came[:, part], 1)[:, None]
            for part in (slice(0, middle // 2), slice(middle // 2, middle))
        ]

        wide_shard = jnp.concatenate([up_weight, down_weight], 1).astype(LOWER)
        if move.staged:
            wide_w = lax.all_gather(wide_shard, ("dp", "mp"), axis=0)
        else:
            wide_w = lax.all_gather(
                lax.all_gather(wide_shard, "dp", axis=0, tiled=True), "mp", axis=0
            )
        shards = jnp.concatenate(
            [
                local_qkv.reshape(shard, 3 * half),
                local_out,
                global_qkv.reshape(shard, 3 * half),
                global_out,
            ],
            1,
        ).astype(LOWER)
        if move.staged:
            turned = [shards] + [move.turn(shards, step) for step in (1, 2, 3)]
            first_line, lat_line = [
                jnp.stack([part[:, start : start + 4 * half] for part in turned])
                for start in (0, 4 * half)
            ]
        else:
            first_line, lat_line = shards[:, : 4 * half], shards[:, 4 * half :]
        first_w = move.spread(first_line)
        first_other = [move.swap(piece) for piece in first_w]
        latent_w = move.spread(wait_for(lat_line, first_w[-1]))

        after, lat_one, triple, stats, mixed, attended = attention_forward(
            move, 0, own, tokens, latents, mod_one, first_w, first_other, sizes
        )


        chip_count = groups * lat_count
        images = jnp.repeat(group_image, lat_count)
        own_slice = lambda value: lax.dynamic_slice_in_dim(value, dp * chip_count, chip_count)
        masks = (
            own_slice(images)[:, None],
            images[None],
            latent_keep[None],
            own_slice(latent_keep)[:, None],
        )
        lat_came = move.swap(lat_one)
        lat_triple, lat_in, lat_weight = latent_project(
            move, lat_one, lat_came, gain, latent_w, half
        )
        key_values_line = move.line(lat_triple)
        key_values = move.spread(key_values_line, chips=True)

        part = own // 2
        ff = token_feed_forward(
            move, 0, part, after, token_cotangent, mod_two, wide_w, sizes, after=[key_values_line]
        )
        lat_mixed, lat_stats, branch_own, branch_other = latent_forward(
            move, lat_triple, key_values, lat_weight, masks, half, features, after=[ff[6]]
        )
        lat_result, grad_lat_two, lat_inputs, lat_narrow, lat_hidden, lat_upward, lat_vec = (
            latent_feed_forward(
                move,
                lat_one,
                branch_own,
                move.swap(branch_other),
                latent_cotangent,
                mod_two,
                wide_w,
                sizes,
            )
        )

        sent, grad_query, out_grad = latent_backward(
            move,
            lat_triple,
            key_values,
            lat_weight,
            masks,
            lat_mixed,
            lat_stats,
            grad_lat_two,
            move.swap(grad_lat_two),
            half,
            features,
        )
        came_line = move.line(sent)
        came = move.spread(came_line, chips=True)
        ff = token_feed_forward(
            move, part, own - part, after, token_cotangent, mod_two, wide_w, sizes, ff, [sent]
        )
        token_result, grad_tok, ff_inputs, ff_narrow, ff_hidden, ff_upward, ff_vec, token_output = ff
        wide_parts = wide_gradients(
            move, 0, ff_inputs, ff_upward, lat_inputs, lat_upward, after=[came_line]
        )
        wide_parts = wide_gradients(
            move, 1, ff_narrow, ff_hidden, lat_narrow, lat_hidden, [wide_parts], came[1:]
        )
        if move.staged:
            wide_sum = lax.psum_scatter(wide_parts, ("mp", "dp"), scatter_dimension=0, tiled=True)
        else:
            wide_sum = lax.psum_scatter(wide_parts, "mp", scatter_dimension=0, tiled=True)
            wide_sum = lax.psum_scatter(
                wide_sum.astype(UPPER), "dp", scatter_dimension=0, tiled=True
            )
        wide_sum = wide_sum.astype(UPPER)
        lat_grad_own, lat_grad_other, gain_rows, early_parts = latent_sources(
            move,
            lat_triple,
            key_values,
            came,
            lat_weight,
            masks,
            grad_query,
            lat_in,
            out_grad,
            lat_one,
            lat_came,
            gain,
            half,
            features,
            after=[wide_parts],
        )
        early_line = move.square_to_line(early_parts)
        grad_lat_one, grad_att, gate_vec = attention_entry(
            move,
            lat_grad_own,
            move.swap(lat_grad_other),
            lat_one,
            grad_lat_two,
            gain,
            mod_one,
            grad_tok,
            attended,
            sizes,
        )

        token_output = fill(move, token_output, move.swap(token_result), [wide_parts])

        grad_tokens, grad_latents, first_in, first_triples, vec_one, grad_output = attention_backward(
            move,
            0,
            own,
            tokens,
            latents,
            mod_one,
            grad_tok,
            grad_lat_one,
            grad_att,
            (triple, stats),
            first_w,
            first_other,
            sizes,
            after=[token_output],
        )
        vec_two = ff_vec + lat_vec
        vectors = jnp.concatenate(
            [vec_one[:, 0], vec_one[:, 1], gate_vec[:, 0]]
            + [vec_two[:, i] for i in range(3)]
            + [gain_rows],
            0,
        ).astype(LOWER)
        vectors_line = move.line(vectors)
        first_factors = (first_in, first_triples, grad_att, mixed, half)
        early_line = move.square_sums(wait_for(early_line, vectors))
        (first_grads_other,) = attention_gradients(
            move, 1, *first_factors, after=[vectors, early_line]
        )
        first_parts = attention_gradients(
            move, 0, *first_factors, [move.swap(first_grads_other)], [vectors_line]
        )
        first_terms = move.meet(first_parts)
        early_sum = move.line_to_own(wait_for(early_line, first_parts[0]))
        mod_grad, grad_terms = modulation_gradients(
            move,
            picked,
            move.spread(vectors_line, chips=True),
            modulator,
            dp_size,
            after=[first_parts[0]],
        )
        first_sums = move.fold(wait_for(first_terms, mod_grad))
        first_sum = move.finish(first_sums)
        grad_output = fill(move, grad_output, move.swap(grad_tokens), [first_sums[-1]])
        mod_grad = mod_grad + move.swap(mod_grad)
        grad_scaled = lax.all_to_all(grad_terms, "dp", 0, 0, tiled=True)
        grad_scaled = grad_scaled.transpose(1, 0, 2).reshape(own, features)
        grad_scaled = move.in_order(grad_scaled, move.swap(grad_scaled))
        grad_condition = jax.vjp(jax.nn.silu, condition)[1](grad_scaled)[0]
        bias_all = mod_grad[shard]
        gain_grad = lax.dynamic_slice_in_dim(mod_grad[shard + 1, :features], dp * shard, shard)
        piece = width // dp_size
        latent_output = move.in_order(lat_result, move.swap(lat_result))
        return (
            token_output,
            latent_output,
            grad_output,
            move.in_order(grad_latents, move.swap(grad_latents)),
            grad_condition,
            mod_grad[:shard],
            lax.dynamic_slice_in_dim(bias_all, dp * piece, piece),
            first_sum[:, : 3 * half].reshape(shard, 3, half),
            first_sum[:, 3 * half :],
            early_sum[:, : 3 * half].reshape(shard, 3, half),
            early_sum[:, 3 * half : 4 * half],
            gain_grad,
            wide_sum[:, :units],
            wide_sum[:, units:],
        )

    return body


def solution(mesh):
    rows, heads = P("dp", None), P("dp", None, "mp")
    columns, vector = P("dp", "mp"), P("dp")
    return jax.shard_map(
        make_body(mesh.shape["dp"]),
        mesh=mesh,
        in_specs=(
            rows, rows, rows, rows, vector, heads, columns, heads, columns, vector,
            columns, columns, P(), P(), rows, rows,
        ),
        out_specs=(
            rows, rows, rows, rows, rows, rows, vector, heads, columns, heads, columns,
            vector, columns, columns,
        ),
        check_vma=False,
    )
```
